32 devices in a mesh: dp: 8 (over z, x), mp: 4 (over y, core).
Axes of the slice: x: 2, y: 2, z: 4, core: 2. Of those that a mesh axis runs over, the one named last changes fastest.
Arguments:
- inputs: float32 [768, 16384], P('mp', 'dp'), may hold values from -6 to 6
- history: float32 [4, 768, 16384], P(None, 'mp', 'dp'), may hold values from -6 to 6
- segment_ids: int32 [16, 1024], P('dp'), may hold values from 0 to 5, never falling along the last dimension, each value on 1 to 512 neighbouring positions
- cotangent: float32 [768, 16384], P('mp', 'dp'), may hold values from -14 to 14
- input_weight: float32 [2, 3, 768, 768], P(None, None, 'mp'), may hold values from -0.21875 to 0.21875
- input_bias: float32 [2, 3, 768], P(None, None, 'mp'), may hold values from -4 to 4
- merge_weight: float32 [2, 768, 768], P(None, 'mp'), may hold values from -0.875 to 0.875
- merge_bias: float32 [2, 768], P(None, 'mp'), may hold values from -4 to 4
- first_gain: float32 [2, 768], P(None, 'mp'), may hold values from 0.25 to 1.75
- first_shift: float32 [2, 768], P(None, 'mp'), may hold values from -4 to 4
- second_gain: float32 [2, 768], P(None, 'mp'), may hold values from 0.25 to 1.75
- second_shift: float32 [2, 768], P(None, 'mp'), may hold values from -4 to 4
- expand_weight: float32 [2, 768, 3072], P(None, None, 'mp'), may hold values from -0.21875 to 0.21875
- expand_bias: float32 [2, 3072], P(None, 'mp'), may hold values from -4 to 4
- reduce_weight: float32 [2, 3072, 768], P(None, 'mp'), may hold values from -0.109375 to 0.109375
- reduce_bias: float32 [2, 768], P(None, 'mp'), may hold values from -4 to 4
- depth_weights: float32 [2, 5], replicated, may hold values from 0.2 to 0.8
Outputs:
- output: float32 [768, 16384], P('mp', 'dp')
- input_grad: float32 [768, 16384], P('mp', 'dp')
- history_grad: float32 [4, 768, 16384], P(None, 'mp', 'dp')
- input_weight_grad: float32 [2, 3, 768, 768], P(None, None, 'mp')
- input_bias_grad: float32 [2, 3, 768], P(None, None, 'mp')
- merge_weight_grad: float32 [2, 768, 768], P(None, 'mp')
- merge_bias_grad: float32 [2, 768], P(None, 'mp')
- first_gain_grad: float32 [2, 768], P(None, 'mp')
- first_shift_grad: float32 [2, 768], P(None, 'mp')
- second_gain_grad: float32 [2, 768], P(None, 'mp')
- second_shift_grad: float32 [2, 768], P(None, 'mp')
- expand_weight_grad: float32 [2, 768, 3072], P(None, None, 'mp')
- expand_bias_grad: float32 [2, 3072], P(None, 'mp')
- reduce_weight_grad: float32 [2, 3072, 768], P(None, 'mp')
- reduce_bias_grad: float32 [2, 768], P(None, 'mp')
- depth_weights_grad: float32 [2, 5], replicated
The draws below stay inside these ranges and needn't reach their ends.
Inputs may be any that keep to these rules, and one draw needn't show every extreme that they name: `segment_ids`: along each packed row the segment numbers never fall.
All inputs are finite; a program needn't handle non-finite values.
Results may differ from the reference program's by a relative error of at most 0.023.
Values may be sent and summed in bfloat16 or wider, within the bound.
No kernel may reach another device: no remote copies, remote signals or barrier semaphores. Data moves between devices by JAX's collectives and lax.ppermute only.
A program may use at most 256 MiB of HBM per device.

```python
import math
import jax
import jax.numpy as jnp
import numpy as np
from jax import lax

D = 768
HEADS = 12
FF = 3072
HEAD = 64
SEQ_LEN = 1024
LAYERS = 2
HISTORY = 4
DOCS = 6
SEQS = 16
TOKENS = 16384


def draw_cotangent(key, part):
    key = jax.random.fold_in(key, 7)
    noise_key = jax.random.fold_in(key, 0)
    row_rise = jnp.arange(TOKENS, dtype=jnp.float32) / max(TOKENS - 1, 1)
    noise_part = jnp.clip(jax.random.normal(noise_key, (D, TOKENS), jnp.float32), -6.0, 6.0)
    return noise_part * (0.5 + row_rise)[None, :]


def levels(stream_key, shape, cuts, least, top_value):
    level = 1.0
    for dim, shards_of in cuts:
        heights = jax.random.uniform(jax.random.fold_in(jax.random.fold_in(stream_key, 6), dim), (shards_of,), jnp.float32, least / len(cuts), top_value / len(cuts))
        level = level * jnp.repeat(jnp.exp(heights), shape[dim] // shards_of).reshape((-1,) + (1,) * (len(shape) - 1 - dim))
    return level


def length_profile(count, total, most, skew):
    loads = [(1 << 20) // math.isqrt(rank ** skew) + 1 for rank in range(2, count + 1)]
    spare, counts = total - most - (count - 1), [1] * (count - 1)
    while spare > 0:
        candidates = [i for i in range(count - 1) if counts[i] < most]
        whole, remaining = sum([loads[i] for i in candidates]), spare
        for i in candidates:
            extra = min(most - counts[i], max(1, remaining * loads[i] // whole), spare)
            counts[i] = counts[i] + extra
            spare = spare - extra
    return np.array([most] + counts)


def ragged_sizes(key, amount, total, bound, skew):
    if amount == 2:
        one = jax.random.randint(key, (), max(1, total - bound), min(bound, total - 1) + 1)
        return jnp.stack([one, total - one])
    lengths = jnp.asarray(length_profile(amount, total, bound, skew), jnp.int32)
    couples = (amount - 1) // 2
    donor, receiver = lengths[1:1 + 2 * couples:2], lengths[2:2 + 2 * couples:2]
    room = jnp.minimum(donor - 1, bound - receiver)
    moved = jax.random.randint(jax.random.fold_in(key, 1), (couples,), 0, 1 << 20) % (room + 1)
    lengths = lengths.at[1:1 + 2 * couples:2].set(donor - moved).at[2:2 + 2 * couples:2].set(receiver + moved)
    return lengths[jax.random.permutation(jax.random.fold_in(key, 2), amount)]


def centred(rng, dims, width, reach, pieces=(), kind=jnp.bfloat16):
    drawn = jax.random.normal(rng, dims, jnp.float32) * width
    if len(pieces) > 0:
        drawn = levels(rng, dims, pieces, -0.22, 0.18) * drawn
    return jnp.clip(drawn, min=-reach, max=reach).astype(kind)


def setup_inputs(seed: int = 0) -> dict:
    key_list = jax.random.split(jax.random.key(seed), 18)
    inputs = centred(key_list[0], (D, TOKENS), 1.0, 6.0, ((0, 4), (1, 8)), jnp.float32)
    history = centred(key_list[1], (HISTORY, D, TOKENS), 1.0, 6.0, ((1, 4), (2, 8)), jnp.float32)
    segment_ids = jax.vmap(lambda own: jnp.searchsorted(jnp.cumsum(ragged_sizes(own, DOCS, SEQ_LEN, SEQ_LEN // 2, 2)), jnp.arange(SEQ_LEN), side="right"))(jax.random.split(key_list[2], SEQS)).reshape((SEQS, SEQ_LEN)).astype(jnp.int32)
    cotangent = draw_cotangent(jax.random.fold_in(key_list[17], 71), 0)
    input_weight = centred(key_list[4], (LAYERS, 3, D, D), D ** -0.5, 0.21875, ((2, 4),), jnp.float32)
    input_bias = centred(key_list[5], (LAYERS, 3, D), 0.3, 4.0, ((2, 4),), jnp.float32)
    merge_weight = centred(key_list[6], (LAYERS, D, D), (D // 16) ** -0.5, 0.875, ((1, 4),), jnp.float32)
    merge_bias = centred(key_list[7], (LAYERS, D), 0.3, 4.0, ((1, 4),), jnp.float32)
    first_gain = jnp.clip(1.0 + 0.15 * jax.random.normal(key_list[8], (LAYERS, D), jnp.float32), 0.25, 1.75)
    first_shift = centred(key_list[9], (LAYERS, D), 0.3, 4.0, ((1, 4),), jnp.float32)
    second_gain = jnp.clip(1.0 + 0.15 * jax.random.normal(key_list[10], (LAYERS, D), jnp.float32), 0.25, 1.75)
    second_shift = centred(key_list[11], (LAYERS, D), 0.3, 4.0, ((1, 4),), jnp.float32)
    expand_weight = centred(key_list[12], (LAYERS, D, FF), D ** -0.5, 0.21875, ((2, 4),), jnp.float32)
    expand_bias = centred(key_list[13], (LAYERS, FF), 0.3, 4.0, ((1, 4),), jnp.float32)
    reduce_weight = centred(key_list[14], (LAYERS, FF, D), FF ** -0.5, 0.109375, ((1, 4),), jnp.float32)
    reduce_bias = centred(key_list[15], (LAYERS, D), 0.3, 4.0, ((1, 4),), jnp.float32)
    depth_weights = jnp.clip(jax.random.uniform(key_list[16], (LAYERS, HISTORY + 1), jnp.float32, 0.2, 0.8), 0.2, 0.8)
    return {"inputs": inputs, "history": history, "segment_ids": segment_ids, "cotangent": cotangent, "input_weight": input_weight, "input_bias": input_bias, "merge_weight": merge_weight, "merge_bias": merge_bias, "first_gain": first_gain, "first_shift": first_shift, "second_gain": second_gain, "second_shift": second_shift, "expand_weight": expand_weight, "expand_bias": expand_bias, "reduce_weight": reduce_weight, "reduce_bias": reduce_bias, "depth_weights": depth_weights}


@jax.custom_vjp
def low(v):
    return lax.optimization_barrier(v.astype(jnp.bfloat16)).astype(jnp.float32)

@jax.custom_vjp
def low_back(v):
    return v

def low_keep(v):
    return (low(v), None)

def low_pass(kept, grad):
    return (grad,)

def back_keep(v):
    return (v, None)

def back_low(kept, grad):
    return (low(grad),)
low.defvjp(low_keep, low_pass)
low_back.defvjp(back_keep, back_low)
EPS = 1e-05
MASKED = -1e+30

def layer_norm(values, gain, shift):
    row_mean = lax.optimization_barrier(jnp.mean(values, -1, keepdims=True))
    variance = lax.optimization_barrier(jnp.mean(values * values, -1, keepdims=True)) - row_mean * row_mean
    return (values - row_mean) * lax.rsqrt(variance + EPS) * gain + shift

def rotary_tables():
    positions = jnp.arange(SEQ_LEN, dtype=jnp.float32)
    frequency = 10000.0 ** (-jnp.arange(HEAD // 2, dtype=jnp.float32) * 2.0 / HEAD)
    angles = positions[:, None] * frequency[None, :]
    return (jnp.cos(angles)[:, None, :], jnp.sin(angles)[:, None, :])

def rotate(values, cosine, sine):
    first = values[..., :HEAD // 2]
    second = values[..., HEAD // 2:]
    return jnp.concatenate([first * cosine - second * sine, second * cosine + first * sine], -1)

def attend_one(items):
    query, key_rot, value_low, segments = items
    scores = jnp.einsum('qhd,khd->hqk', query, key_rot, precision=lax.Precision.HIGHEST) * HEAD ** (-0.5)
    scores = low_back(scores)
    positions = jnp.arange(SEQ_LEN)
    allowed = (segments[:, None] == segments[None, :]) & (positions[None, :] <= positions[:, None])
    scores = jnp.where(allowed[None], scores, MASKED)
    peak = lax.optimization_barrier(jnp.max(scores, -1, keepdims=True))
    weights = jnp.exp(scores - peak)
    probs = weights / lax.optimization_barrier(jnp.sum(weights, -1, keepdims=True))
    return jnp.einsum('hqk,khd->qhd', low(probs), value_low, precision=lax.Precision.HIGHEST)

def product(left, right):
    return jnp.dot(left, right, precision=lax.Precision.HIGHEST, preferred_element_type=jnp.float32)

def block(values, segment_ids, layer, tables):
    w_input, b_input, w_merge, b_merge, gain_one, shift_one, gain_two, shift_two, w_expand, b_expand, w_reduce, b_reduce = layer
    cosine, sine = tables
    normed = low(layer_norm(values, gain_one, shift_one))
    projected = low_back(jnp.einsum('td,kfd->tkf', normed, low(w_input), precision=lax.Precision.HIGHEST)) + b_input[None]
    parts = projected.reshape(SEQS, SEQ_LEN, 3, HEADS, HEAD)
    query = low(rotate(parts[:, :, 0], cosine, sine))
    key_rot = low(rotate(parts[:, :, 1], cosine, sine))
    value_low = low(parts[:, :, 2])
    attended = lax.map(jax.checkpoint(attend_one), (query, key_rot, value_low, segment_ids))
    attended = low(low_back(attended.reshape(TOKENS, D)))
    middle = values + low_back(product(attended, low(w_merge))) + b_merge
    normed_two = low(layer_norm(middle, gain_two, shift_two))
    activated = low(jax.nn.gelu(low_back(product(normed_two, low(w_expand))) + b_expand))
    return middle + low_back(product(activated, low(w_reduce))) + b_reduce

def model(inputs, history, segment_ids, stacks, depth_weights):
    tables = rotary_tables()
    current = inputs
    outputs_list = []
    for index in range(LAYERS):
        layer = tuple((item[index] for item in stacks))
        outputs_list.append(block(current, segment_ids, layer, tables))
        entries = [history[j] for j in range(index, HISTORY)] + outputs_list
        mixed = depth_weights[index, 0] * entries[0]
        for j in range(1, len(entries)):
            mixed = mixed + depth_weights[index, j] * entries[j]
        current = mixed
    return current

def reference(inputs, history, segment_ids, cotangent, input_weight, input_bias, merge_weight, merge_bias, first_gain, first_shift, second_gain, second_shift, expand_weight, expand_bias, reduce_weight, reduce_bias, depth_weights):

    def forward(inputs, history, input_weight, input_bias, merge_weight, merge_bias, first_gain, first_shift, second_gain, second_shift, expand_weight, expand_bias, reduce_weight, reduce_bias, depth_weights):
        stacks = (input_weight, input_bias, merge_weight, merge_bias, first_gain, first_shift, second_gain, second_shift, expand_weight, expand_bias, reduce_weight, reduce_bias)
        result = model(jnp.transpose(inputs), jnp.transpose(history, (0, 2, 1)), segment_ids, stacks, depth_weights)
        return jnp.transpose(result)
    output, pullback = jax.vjp(forward, inputs, history, input_weight, input_bias, merge_weight, merge_bias, first_gain, first_shift, second_gain, second_shift, expand_weight, expand_bias, reduce_weight, reduce_bias, depth_weights)
    grads = pullback(cotangent)
    return (output, grads[0], grads[1], grads[2], grads[3], grads[4], grads[5], grads[6], grads[7], grads[8], grads[9], grads[10], grads[11], grads[12], grads[13], grads[14])
```

```python
import functools

import jax
import jax.numpy as jnp
from jax import lax
from jax.experimental import pallas as pl
from jax.experimental.pallas import tpu as pltpu
from jax.sharding import PartitionSpec as P

HEAD = 64
HALF = HEAD // 2
LAYERS = 2
HISTORY = 4
EPS = 1e-05
MASKED = -1e30
BLK = 256
REACH = 512
TILE = 256
STRIP = 96
BF = jnp.bfloat16
F32 = jnp.float32
GELU_A = 0.7978845608028654
GELU_B = 0.044715
GAIN1, SHIFT1, GAIN2, SHIFT2, MERGE_B, REDUCE_B, INPUT_B, EXPAND_B = 0, 1, 2, 3, 4, 5, 6, 8


def dot(a, b, on):
    return lax.dot_general(a, b, (on, ((), ())), preferred_element_type=F32)


def nn(a, b):
    return dot(a, b, ((1,), (0,)))


def nt(a, b):
    return dot(a, b, ((1,), (1,)))


def tn(a, b):
    return dot(a, b, ((0,), (0,)))


def full(shape):
    return pl.BlockSpec(shape, lambda t: (0,) * len(shape))


def shape(dims, kind=BF):
    return jax.ShapeDtypeStruct(dims, kind)


def launch(kernel, name, steps, ins, outs, scratch, micros, vmem):
    return pl.pallas_call(
        kernel,
        grid=(steps,),
        in_specs=[spec for _, spec in ins],
        out_specs=[spec for _, spec in outs],
        out_shape=[struct for struct, _ in outs],
        scratch_shapes=scratch,
        compiler_params=pltpu.CompilerParams(
            dimension_semantics=("arbitrary",), vmem_limit_bytes=vmem * 1024 * 1024
        ),
        cost_estimate=pl.CostEstimate(
            flops=int(micros * 1.0e9), bytes_accessed=1 << 20, transcendentals=0
        ),
        name=name,
    )(*[operand for operand, _ in ins])


def whole(*operands):
    return [(operand, full(operand.shape)) for operand in operands]


def scalars(operand):
    return [(operand, pl.BlockSpec(memory_space=pltpu.SMEM))]


def out_full(dims, kind=BF):
    return (shape(dims, kind), full(dims))


def strips(size):
    return [slice(at, at + STRIP) for at in range(0, size, STRIP)]


def key_range(block):
    return max(0, block * BLK - REACH), (block + 1) * BLK


def mask_shape(length):
    return (length // BLK, min(length, REACH + BLK), BLK)


def fill_mask(mask, segments, length):
    line = segments[...]
    column = jnp.broadcast_to(line, (8, length)).T[:, 0:1]
    for block in range(length // BLK):
        low, high = key_range(block)
        span = high - low
        here = line[:, block * BLK : high]
        there = column[low:high, :]
        query_pos = lax.broadcasted_iota(jnp.int32, (span, BLK), 1) + block * BLK
        key_pos = lax.broadcasted_iota(jnp.int32, (span, BLK), 0) + low
        allowed = (here == there) & (key_pos <= query_pos)
        mask[block, :span, :] = jnp.where(allowed, 0.0, MASKED)


def normalise(source, target, stats, columns, gain, shift, width, length):
    total = jnp.zeros((1, length), F32)
    squares = jnp.zeros((1, length), F32)
    for rows in strips(width):
        x = source(rows)
        total += jnp.sum(x, 0, keepdims=True)
        squares += jnp.sum(x * x, 0, keepdims=True)
    mean = total * (1.0 / width)
    scale = lax.rsqrt(squares * (1.0 / width) - mean * mean + EPS)
    stats[0:1, :] = mean
    stats[1:2, :] = scale
    return mean, scale


def apply_norm(x, mean, scale, columns, gain, shift, rows):
    return ((x - mean) * scale * columns[rows, gain : gain + 1] + columns[rows, shift : shift + 1]).astype(BF)


def norm_back(x, stats, left, right, base, gain, width, length, grad_n, grad_gain, emit):
    mean, scale = stats[0:1, :], stats[1:2, :]
    first = jnp.zeros((1, length), F32)
    second = jnp.zeros((1, length), F32)
    for rows in strips(width):
        hat = (x[rows, :].astype(F32) - mean) * scale
        grad = left[rows, :].astype(F32) + right[rows, :].astype(F32)
        grad_n[rows, :] = grad.astype(BF)
        product = grad * hat
        grad_gain[rows, :] = product.astype(BF)
        column = gain[rows]
        first += jnp.sum(grad * column, 0, keepdims=True)
        second += jnp.sum(product * column, 0, keepdims=True)
    first = first * (1.0 / width)
    second = second * (1.0 / width)
    for rows in strips(width):
        hat = (x[rows, :].astype(F32) - mean) * scale
        grad = left[rows, :].astype(F32) + right[rows, :].astype(F32)
        emit(rows, base(rows) + scale * (grad * gain[rows] - first - hat * second))


def row_sums(value):
    return nt(jnp.ones((8, value.shape[1]), BF), value)


def attention_forward_kernel(mixing, heads, length, width, *refs):
    refs = list(refs)
    if mixing:
        coef, history_i, mid_i, left, right, before = refs[:6]
        del refs[:6]
    else:
        x_i = refs.pop(0)
    vectors, a0d, a0r, a1d, a1r, cos, sin, segments = refs[:8]
    del refs[:8]
    if mixing:
        y_o, x_o = refs[:2]
        del refs[:2]
    n1_o, st_o, q_o, k_o, v_o, o_o, lse_o, part_o, lin, mask, o_all = refs
    head = pl.program_id(0)
    quarter = (heads // 2) * HEAD
    half = width // 2

    @pl.when(head == 0)
    def _():
        columns = vectors[...].T
        if mixing:
            bias = before[...].T
            weight = coef[0, HISTORY]
            for rows in strips(width):
                y = (
                    mid_i[rows, :].astype(F32)
                    + left[rows, :].astype(F32)
                    + right[rows, :].astype(F32)
                    + bias[rows, REDUCE_B : REDUCE_B + 1]
                )
                y_o[rows, :] = y.astype(BF)
                x_o[rows, :] = (history_i[rows, :].astype(F32) + weight * y).astype(BF)
            source = x_o
        else:
            source = x_i
        mean, scale = normalise(
            lambda rows: source[rows, :].astype(F32), None, st_o, None, None, None, width, length
        )
        for rows in strips(width):
            n1_o[rows, :] = apply_norm(
                source[rows, :].astype(F32), mean, scale, columns, GAIN1, SHIFT1, rows
            )
        for index, (d, r) in enumerate(((a0d, a0r), (a1d, a1r))):
            at = index * 3 * quarter
            lin[at : at + 3 * quarter, :] = (
                nn(d[: 3 * quarter, :], n1_o[:half, :])
                + nn(r[: 3 * quarter, :], n1_o[half:, :])
                + columns[: 3 * quarter, INPUT_B + index : INPUT_B + index + 1]
            )
        fill_mask(mask, segments, length)

    c, s = cos[...], sin[...]
    group = head // (heads // 2)
    base = group * 3 * quarter + (head - group * (heads // 2)) * HEAD

    def rope(start):
        first = lin[pl.ds(pl.multiple_of(start, HALF), HALF), :]
        second = lin[pl.ds(pl.multiple_of(start + HALF, HALF), HALF), :]
        return jnp.concatenate([first * c - second * s, second * c + first * s], 0)

    q = (rope(base).astype(BF) * BF(HEAD**-0.5)).astype(BF)
    key = rope(base + quarter).astype(BF)
    v = lin[pl.ds(pl.multiple_of(base + 2 * quarter, HEAD), HEAD), :].astype(BF)
    q_o[0] = q
    k_o[0] = key
    v_o[0] = v
    for block in range(length // BLK):
        low, high = key_range(block)
        cols = slice(block * BLK, high)
        scores = tn(key[:, low:high], q[:, cols]) + mask[block, : high - low, :]
        peak = jnp.max(scores, 0, keepdims=True)
        weights = jnp.exp(scores - peak)
        total = jnp.sum(weights, 0, keepdims=True)
        out = (nn(v[:, low:high], weights.astype(BF)) * (1.0 / total)).astype(BF)
        o_o[0, :, cols] = out
        o_all[pl.ds(pl.multiple_of(head * HEAD, HEAD), HEAD), cols] = out
        lse_o[0, :, cols] = peak + jnp.log(total)

    @pl.when(head == heads - 1)
    def _():
        for at, own, other in ((0, a0d, a1d), (half, a0r, a1r)):
            part_o[at : at + half, :] = (
                tn(own[3 * quarter :, :], o_all[:quarter, :])
                + tn(other[3 * quarter :, :], o_all[quarter:, :])
            ).astype(BF)


def attention_forward(mix, x, vectors, weights, cos, sin, segments):
    length = segments.shape[1]
    rows, half = weights[0].shape
    width = 2 * half
    quarter = rows // 4
    heads = 2 * quarter // HEAD
    if mix is not None:
        ins = scalars(mix[0]) + whole(*mix[1:])
        outs = [out_full((width, length)), out_full((width, length))]
    else:
        ins = whole(x)
        outs = []
    ins = ins + whole(vectors, *weights, cos, sin, segments)
    per_head = lambda size: pl.BlockSpec((1, size, length), lambda h: (h, 0, 0))
    heads_out = (shape((heads, HEAD, length)), per_head(HEAD))
    outs = outs + [
        out_full((width, length)),
        out_full((8, length), F32),
        heads_out,
        heads_out,
        heads_out,
        heads_out,
        (shape((heads, 1, length), F32), per_head(1)),
        out_full((width, length)),
    ]
    return launch(
        functools.partial(attention_forward_kernel, mix is not None, heads, length, width),
        "attention_forward",
        heads,
        ins,
        outs,
        [
            pltpu.VMEM((6 * quarter, length), F32),
            pltpu.VMEM(mask_shape(length), F32),
            pltpu.VMEM((2 * quarter, length), BF),
        ],
        20,
        44,
    )


def attention_backward_kernel(opening, heads, length, width, *refs):
    refs = list(refs)
    if opening:
        grad_i, left, right, mid, st, vectors = refs[:6]
        del refs[:6]
    else:
        gmb = refs.pop(0)
    n1, ad, ar, cos, sin, segments, q_i, k_i, v_i, o_i, lse_i = refs[:11]
    del refs[:11]
    if opening:
        gmb, sums_o = refs[:2]
        del refs[:2]
    else:
        add = refs.pop(0)
    dw_o, db_o, part_o, mask, go_all, gl_all, gk_s, gv_s = refs[:8]
    del refs[:8]
    head = pl.program_id(0)
    quarter = heads * HEAD
    half = width // 2

    @pl.when(head == 0)
    def _():
        if opening:
            grad_n, grad_gain = refs
            columns = vectors[...].T
            norm_back(
                mid,
                st,
                left,
                right,
                lambda rows: grad_i[rows, :].astype(F32),
                columns[:, GAIN2 : GAIN2 + 1],
                width,
                length,
                grad_n,
                grad_gain,
                lambda rows, value: gmb.__setitem__((rows, slice(None)), value.astype(BF)),
            )
            sums_o[0:8, :] = row_sums(grad_gain[...])
            sums_o[8:16, :] = row_sums(grad_n[...])
            sums_o[16:24, :] = row_sums(gmb[...])
        go_all[...] = (
            nn(ad[3 * quarter :, :], gmb[:half, :]) + nn(ar[3 * quarter :, :], gmb[half:, :])
        ).astype(BF)
        o_flat = o_i[...].reshape(quarter, length)
        dw_o[0, 3 * quarter :, :] = nt(o_flat, gmb[:half, :]).astype(BF)
        dw_o[1, 3 * quarter :, :] = nt(o_flat, gmb[half:, :]).astype(BF)
        fill_mask(mask, segments, length)

    base = pl.multiple_of(head * HEAD, HEAD)
    q, key, v = q_i[0], k_i[0], v_i[0]
    go = go_all[pl.ds(base, HEAD), :]
    delta = jnp.sum(go.astype(F32) * o_i[head].astype(F32), 0, keepdims=True)
    gk_s[...] = jnp.zeros_like(gk_s)
    gv_s[...] = jnp.zeros_like(gv_s)
    gq_parts = []
    for block in range(length // BLK):
        low, high = key_range(block)
        cols = slice(block * BLK, high)
        scores = tn(key[:, low:high], q[:, cols]) + mask[block, : high - low, :]
        probs = jnp.exp(scores - lse_i[0, :, cols])
        grad_probs = tn(v[:, low:high], go[:, cols])
        grad_scores = (probs * (grad_probs - delta[:, cols])).astype(BF)
        gv_s[:, low:high] += nt(go[:, cols], probs.astype(BF))
        gk_s[:, low:high] += nt(q[:, cols], grad_scores)
        gq_parts.append(nn(key[:, low:high], grad_scores))
    c, s = cos[...], sin[...]

    def store(part, top, bottom):
        start = pl.multiple_of(part * quarter + base, HEAD)
        gl_all[pl.ds(start, HEAD), :] = jnp.concatenate([top, bottom], 0).astype(BF)

    gq = jnp.concatenate(gq_parts, 1) * HEAD**-0.5
    store(0, gq[:HALF] * c + gq[HALF:] * s, gq[HALF:] * c - gq[:HALF] * s)
    gk = gk_s[...]
    store(1, gk[:HALF] * c + gk[HALF:] * s, gk[HALF:] * c - gk[:HALF] * s)
    store(2, gv_s[:HALF, :], gv_s[HALF:, :])

    @pl.when(head == heads - 1)
    def _():
        db_o[...] = row_sums(gl_all[...])
        dw_o[0, : 3 * quarter, :] = nt(gl_all[...], n1[:half, :]).astype(BF)
        dw_o[1, : 3 * quarter, :] = nt(gl_all[...], n1[half:, :]).astype(BF)
        for at, w in ((0, ad), (half, ar)):
            value = tn(w[: 3 * quarter, :], gl_all[...])
            if not opening:
                value = value + add[at : at + half, :]
            part_o[at : at + half, :] = value.astype(part_o.dtype)


def attention_backward(opening, gmb, n1, weights, cos, sin, segments, saved, group, add):
    length = segments.shape[1]
    rows, half = weights[0].shape
    width = 2 * half
    quarter = rows // 4
    heads = quarter // HEAD
    q, key, v, o, lse = saved
    if opening is not None:
        ins = whole(*opening)
        outs = [out_full((width, length)), out_full((24, width), F32)]
        scratch = [pltpu.VMEM((width, length), BF), pltpu.VMEM((width, length), BF)]
    else:
        ins = whole(gmb)
        outs = []
        scratch = []
    at = group * heads
    per_head = lambda size: pl.BlockSpec((1, size, length), lambda h: (at + h, 0, 0))
    ins = ins + whole(n1, *weights, cos, sin, segments)
    ins = ins + [(item, per_head(HEAD)) for item in (q, key, v)]
    ins = ins + [(o, pl.BlockSpec((heads, HEAD, length), lambda h: (group, 0, 0))), (lse, per_head(1))]
    if add is not None:
        ins = ins + whole(add)
    outs = outs + [
        out_full((2, rows, half)),
        out_full((8, 3 * quarter), F32),
        out_full((width, length), BF if add is not None else F32),
    ]
    return launch(
        functools.partial(attention_backward_kernel, opening is not None, heads, length, width),
        "attention_backward",
        heads,
        ins,
        outs,
        [
            pltpu.VMEM(mask_shape(length), F32),
            pltpu.VMEM((quarter, length), BF),
            pltpu.VMEM((3 * quarter, length), BF),
            pltpu.VMEM((HEAD, length), F32),
            pltpu.VMEM((HEAD, length), F32),
        ]
        + scratch,
        14,
        44,
    )


def mlp_forward_kernel(tiles, length, width, *refs):
    (x, left, right, vectors, e0d, e0r, e1d, e1r, r0d, r0r, r1d, r1r) = refs[:12]
    mid_o, n2_o, st_o, u_o, act_o, part_o, acts, columns_s = refs[12:]
    t = pl.program_id(0)
    half = width // 2
    units = tiles * TILE

    @pl.when(t == 0)
    def _():
        columns = vectors[...].T
        columns_s[:, : columns.shape[1]] = columns
        for rows in strips(width):
            mid_o[rows, :] = (
                x[rows, :].astype(F32)
                + left[rows, :].astype(F32)
                + right[rows, :].astype(F32)
                + columns[rows, MERGE_B : MERGE_B + 1]
            ).astype(BF)
        mean, scale = normalise(
            lambda rows: mid_o[rows, :].astype(F32), None, st_o, None, None, None, width, length
        )
        for rows in strips(width):
            n2_o[rows, :] = apply_norm(
                mid_o[rows, :].astype(F32), mean, scale, columns, GAIN2, SHIFT2, rows
            )

    def expand(group, d, r):
        at = pl.multiple_of((t - group * tiles) * TILE, TILE)
        bias = columns_s[pl.ds(at, TILE), EXPAND_B + group : EXPAND_B + group + 1]
        u = tn(d[...], n2_o[:half, :]) + tn(r[...], n2_o[half:, :]) + bias
        act = (0.5 * u * (1.0 + jnp.tanh(GELU_A * (u + GELU_B * (u * u * u))))).astype(BF)
        u_o[...] = u.astype(BF)
        act_o[...] = act
        acts[pl.ds(pl.multiple_of(t * TILE, TILE), TILE), :] = act

    @pl.when(t < tiles)
    def _():
        expand(0, e0d, e0r)

    @pl.when(t >= tiles)
    def _():
        expand(1, e1d, e1r)

    @pl.when(t == 2 * tiles - 1)
    def _():
        for at, own, other in ((0, r0d, r1d), (half, r0r, r1r)):
            part_o[at : at + half, :] = (
                tn(own[...], acts[:units, :]) + tn(other[...], acts[units:, :])
            ).astype(BF)


def mlp_forward(x, left, right, vectors, expand, reduce):
    width, length = x.shape
    half, units = expand[0].shape
    tiles = units // TILE
    first = pl.BlockSpec((half, TILE), lambda t: (0, jnp.minimum(t, tiles - 1)))
    second = pl.BlockSpec((half, TILE), lambda t: (0, jnp.maximum(t - tiles, 0)))
    ins = whole(x, left, right, vectors)
    ins = ins + list(zip(expand, (first, first, second, second))) + whole(*reduce)
    per_tile = (shape((2 * units, length)), pl.BlockSpec((TILE, length), lambda t: (t, 0)))
    return launch(
        functools.partial(mlp_forward_kernel, tiles, length, width),
        "mlp_forward",
        2 * tiles,
        ins,
        [
            out_full((width, length)),
            out_full((width, length)),
            out_full((8, length), F32),
            per_tile,
            per_tile,
            out_full((width, length)),
        ],
        [pltpu.VMEM((2 * units, length), BF), pltpu.VMEM((width, 128), F32)],
        14,
        44,
    )


def mlp_backward_kernel(mode, tiles, length, width, *refs):
    refs = list(refs)
    half = width // 2
    units = tiles * TILE
    if mode == "last":
        coef, cot, mid, left, right, y0, vectors = refs[:7]
        del refs[:7]
    elif mode == "first":
        coef, cot, gmid, x, st, left, right, y0, vectors = refs[:9]
        del refs[:9]
    else:
        gyb = refs.pop(0)
    n2, u_i, act, rd, rr, ed, er = refs[:7]
    del refs[:7]
    if mode == "own":
        add = refs.pop(0)
    else:
        gyb = refs.pop(0)
        if mode == "first":
            gx_o = refs.pop(0)
        sums_o, dots_o = refs[:2]
        del refs[:2]
    g_o, be_o, part_o, gubs = refs[:4]
    del refs[:4]
    t = pl.program_id(0)

    if mode != "own":

        @pl.when(t == 0)
        def _():
            columns = vectors[...].T
            dots_o[...] = jnp.zeros_like(dots_o)
            if mode == "last":
                for rows in strips(width):
                    value = cot[rows, :].astype(F32)
                    gyb[rows, :] = (coef[1, HISTORY] * value).astype(BF)
                    y1 = (
                        mid[rows, :].astype(F32)
                        + left[rows, :].astype(F32)
                        + right[rows, :].astype(F32)
                        + columns[rows, REDUCE_B : REDUCE_B + 1]
                    )
                    dots_o[0:1, :] += jnp.sum(value * y0[rows, :].astype(F32), 0, keepdims=True)
                    dots_o[1:2, :] += jnp.sum(value * y1, 0, keepdims=True)
                sums_o[0:8, :] = row_sums(gyb[...])
            else:
                grad_n, grad_gain = refs

                def emit(rows, value):
                    gx_o[rows, :] = value.astype(BF)
                    gyb[rows, :] = (
                        coef[1, HISTORY - 1] * cot[rows, :].astype(F32) + coef[0, HISTORY] * value
                    ).astype(BF)
                    dots_o[0:1, :] += jnp.sum(value * y0[rows, :].astype(F32), 0, keepdims=True)

                norm_back(
                    x,
                    st,
                    left,
                    right,
                    lambda rows: gmid[rows, :].astype(F32),
                    columns[:, GAIN1 : GAIN1 + 1],
                    width,
                    length,
                    grad_n,
                    grad_gain,
                    emit,
                )
                sums_o[0:8, :] = row_sums(gyb[...])
                sums_o[8:16, :] = row_sums(grad_gain[...])
                sums_o[16:24, :] = row_sums(grad_n[...])

    ga = nn(rd[...], gyb[:half, :]) + nn(rr[...], gyb[half:, :])
    u = u_i[...].astype(F32)
    square = u * u
    th = jnp.tanh(GELU_A * u * (1.0 + GELU_B * square))
    slope = 0.5 * (1.0 + th) + (0.5 * GELU_A) * u * (1.0 - th * th) * (1.0 + (3.0 * GELU_B) * square)
    gub = (ga * slope).astype(BF)
    gubs[pl.ds(pl.multiple_of(t * TILE, TILE), TILE), :] = gub
    be_o[...] = row_sums(gub)
    g_o[0, 0] = nt(gub, n2[:half, :]).astype(BF)
    g_o[1, 0] = nt(gub, n2[half:, :]).astype(BF)
    g_o[0, 1] = nt(act[...], gyb[:half, :]).astype(BF)
    g_o[1, 1] = nt(act[...], gyb[half:, :]).astype(BF)

    @pl.when(t == tiles - 1)
    def _():
        for at, w in ((0, ed), (half, er)):
            value = nn(w[...], gubs[...])
            if mode == "own":
                value = value + add[at : at + half, :]
            part_o[at : at + half, :] = value.astype(part_o.dtype)


def mlp_backward(mode, opening, gyb, n2, u, act, group, reduce, expand, add):
    width, length = n2.shape
    half, units = expand[0].shape
    tiles = units // TILE
    outs = []
    scratch = [pltpu.VMEM((units, length), BF)]
    if mode == "own":
        ins = whole(gyb)
    else:
        ins = scalars(opening[0]) + whole(*opening[1:])
        outs = outs + [out_full((width, length))]
        if mode == "first":
            outs = outs + [out_full((width, length))]
            scratch = scratch + [pltpu.VMEM((width, length), BF), pltpu.VMEM((width, length), BF)]
        outs = outs + [out_full((24, width), F32), out_full((8, length), F32)]
    at = group * tiles
    per_tile = pl.BlockSpec((TILE, length), lambda t: (at + t, 0))
    reduce_tile = pl.BlockSpec((TILE, half), lambda t: (t, 0))
    ins = ins + whole(n2) + [(u, per_tile), (act, per_tile)]
    ins = ins + [(item, reduce_tile) for item in reduce] + whole(*expand)
    if add is not None:
        ins = ins + whole(add)
    outs = outs + [
        (shape((2, 2, units, half)), pl.BlockSpec((2, 2, TILE, half), lambda t: (0, 0, t, 0))),
        (shape((8, units), F32), pl.BlockSpec((8, TILE), lambda t: (0, t))),
        out_full((width, length), BF if add is not None else F32),
    ]
    return launch(
        functools.partial(mlp_backward_kernel, mode, tiles, length, width),
        "mlp_backward",
        tiles,
        ins,
        outs,
        scratch,
        13,
        44,
    )


def final_kernel(length, width, gmid, x, st, left, right, vectors, gx_o, sums_o, grad_n, grad_gain):
    columns = vectors[...].T
    norm_back(
        x,
        st,
        left,
        right,
        lambda rows: gmid[rows, :].astype(F32),
        columns[:, GAIN1 : GAIN1 + 1],
        width,
        length,
        grad_n,
        grad_gain,
        lambda rows, value: gx_o.__setitem__((rows, slice(None)), value.astype(BF)),
    )
    sums_o[0:8, :] = row_sums(grad_gain[...])
    sums_o[8:16, :] = row_sums(grad_n[...])


def final_backward(*operands):
    width, length = operands[0].shape
    return launch(
        functools.partial(final_kernel, length, width),
        "norm_backward",
        1,
        whole(*operands),
        [out_full((width, length)), out_full((16, width), F32)],
        [pltpu.VMEM((width, length), BF), pltpu.VMEM((width, length), BF)],
        5,
        32,
    )


def swap_core(value):
    size = lax.axis_size("mp")
    return lax.ppermute(value, "mp", [(i, i ^ 1) for i in range(size)])


def swap_row(value):
    size = lax.axis_size("mp")
    return lax.ppermute(value, "mp", [(i, i ^ 2) for i in range(size)])


def swap_dp(value, bit):
    size = lax.axis_size("dp")
    return lax.ppermute(value, "dp", [(i, i ^ bit) for i in range(size)])


def half_of(value, which, axis=0):
    size = value.shape[axis] // 2
    return lax.dynamic_slice_in_dim(value, which * size, size, axis)


def ordered(mine, theirs, which, axis=0):
    return jnp.where(
        which == 0,
        jnp.concatenate([mine, theirs], axis),
        jnp.concatenate([theirs, mine], axis),
    )


def spread(mine, flip, core):
    theirs = swap_row(mine)
    pair = ordered(mine[None], theirs[None], flip)
    other = swap_core(pair)
    return (
        jnp.where(
            core == 0,
            jnp.stack([pair[0], other[0], pair[1], other[1]]),
            jnp.stack([other[0], pair[0], other[1], pair[1]]),
        ),
        theirs,
    )


def to_row(value, row, core, flip):
    length = value.shape[1] // 2
    low = value.astype(BF)
    mine = lax.dynamic_slice_in_dim(low, row * length, length, 1)
    theirs = swap_row(lax.dynamic_slice_in_dim(low, (1 - row) * length, length, 1))
    pair = ordered(mine[None], theirs[None], flip)
    other = swap_core(pair)
    gathered = jnp.where(
        core == 0,
        jnp.stack([pair[0], other[0], pair[1], other[1]]),
        jnp.stack([other[0], pair[0], other[1], pair[1]]),
    )
    return gathered.reshape(4 * value.shape[0], length)


def from_row(pick, row, core, flip):
    mine = pick(2 * flip + core).astype(BF)
    sent = pick(2 * (1 - flip) + core).astype(BF)
    return ordered(mine, swap_row(sent), row, 1).astype(F32)


def fetch_other(low, bit):
    direct = swap_row(low)
    return direct, swap_dp(direct, 1)


def sum_dp(kept, sent, bits):
    value = (kept.astype(F32) + swap_dp(sent, 1).astype(F32)).astype(BF)
    for step in range(1, len(bits)):
        away = half_of(value, 1 - bits[step])
        value = (
            half_of(value, bits[step]).astype(F32) + swap_dp(away, 1 << step).astype(F32)
        ).astype(BF)
    for step in reversed(range(1, len(bits))):
        value = ordered(value, swap_dp(value, 1 << step), bits[step])
    return value, swap_dp(value, 1)


def add_rows(own, received):
    total = own.astype(F32) + received.astype(F32)
    return total.astype(BF)


def reduce_grad(own, other, bits):
    received = swap_row(other)
    return sum_dp(add_rows(own[0], received[0]), add_rows(own[1], received[1]), bits)


def shards(
    inputs,
    history,
    segment_ids,
    cotangent,
    input_weight,
    input_bias,
    merge_weight,
    merge_bias,
    first_gain,
    first_shift,
    second_gain,
    second_shift,
    expand_weight,
    expand_bias,
    reduce_weight,
    reduce_bias,
    depth_weights,
):
    member = lax.axis_index("mp")
    row, core = member // 2, member % 2
    dp = lax.axis_index("dp")
    bits = []
    size = lax.axis_size("dp")
    while (1 << len(bits)) < size:
        bits.append((dp >> len(bits)) & 1)
    bit = bits[0]
    flip = row ^ bit
    length = segment_ids.shape[1]
    part = inputs.shape[0]
    width = 4 * part
    half = width // 2
    units = expand_bias.shape[1]
    last = HISTORY - 1

    segments = lax.dynamic_slice_in_dim(segment_ids, row, 1, 0).astype(F32)
    frequency = 10000.0 ** (-jnp.arange(HALF, dtype=F32) * 2.0 / HEAD)
    angles = frequency[:, None] * jnp.arange(length, dtype=F32)[None, :]
    cos, sin = jnp.cos(angles), jnp.sin(angles)

    x0 = to_row(inputs, row, core, flip)

    small = jnp.concatenate(
        [
            item.reshape(LAYERS, -1)
            for item in (
                input_bias,
                expand_bias,
                first_gain,
                first_shift,
                second_gain,
                second_shift,
                merge_bias,
                reduce_bias,
            )
        ],
        1,
    )
    quarters, small_other = spread(small, flip, core)
    at = 3 * part + units
    wide = quarters[:, :, at:].reshape(4, LAYERS, 6, part).transpose(1, 2, 0, 3)
    wide = wide.reshape(LAYERS, 6, width)
    pair = jnp.stack([small, small_other], 1)
    input_rows = jnp.pad(pair[:, :, : 3 * part], ((0, 0), (0, 0), (0, width - 3 * part)))
    vectors = jnp.concatenate(
        [wide, input_rows, pair[:, :, 3 * part : at], jnp.zeros((LAYERS, 6, width), F32)], 1
    )

    attn_w, expand_w, reduce_w = [], [], []
    for l in range(LAYERS):
        merged = jnp.concatenate([input_weight[l].reshape(3 * part, width), merge_weight[l]], 0)
        for source, axis, held in (
            (merged, 1, attn_w),
            (expand_weight[l], 0, expand_w),
            (reduce_weight[l], 1, reduce_w),
        ):
            near = half_of(source, bit, axis).astype(BF)
            far = half_of(source, 1 - bit, axis).astype(BF)
            held.append((near, far) + fetch_other(near, bit))

    mixed_history = sum(depth_weights[0, j] * history[j] for j in range(HISTORY))
    hm0 = to_row(mixed_history, row, core, flip)
    cot = to_row(cotangent, row, core, flip)

    saved = []
    mix = None
    for l in range(LAYERS):
        vec = vectors[l]
        outs = attention_forward(
            mix, x0 if l == 0 else None, vec, attn_w[l], cos, sin, segments
        )
        if l == 0:
            x = x0
        else:
            y0, x = outs[:2]
            outs = outs[2:]
        n1, st1, q, k, v, o, lse, left = outs
        right = swap_core(left)
        mid, n2, st2, u, act, left = mlp_forward(x, left, right, vec, expand_w[l], reduce_w[l])
        right = swap_core(left)
        saved.append((x, n1, st1, (q, k, v, o, lse), mid, n2, st2, u, act, left, right))
        mix = (depth_weights, hm0, mid, left, right, vec)

    mid1, left1, right1 = saved[1][4], saved[1][9], saved[1][10]

    def tail_quarter(index):
        cut = lambda item: lax.dynamic_slice_in_dim(item, index * part, part, 0).astype(F32)
        bias = lax.dynamic_slice_in_dim(vectors[1, REDUCE_B], index * part, part, 0)
        y1 = cut(mid1) + cut(left1) + cut(right1) + bias[:, None]
        return depth_weights[1, last] * cut(y0) + depth_weights[1, last + 1] * y1

    output = sum(depth_weights[1, j] * history[j + 1] for j in range(last)) + from_row(
        tail_quarter, row, core, flip
    )

    totals = [None] * LAYERS
    sums = [{} for _ in range(LAYERS)]
    for l in reversed(range(LAYERS)):
        x, n1, st1, heads, mid, n2, st2, u, act, y_left, y_right = saved[l]
        vec = vectors[l]
        aw, ew, rw = attn_w[l], expand_w[l], reduce_w[l]
        if l == 1:
            opening = (depth_weights, cot, mid, y_left, y_right, y0, vec)
            gyb, wide_sums, dots1, g1, be1, partial = mlp_backward(
                "last", opening, None, n2, u, act, 1, rw[2:], ew[2:], None
            )
            sums[1]["reduce_b"] = wide_sums[0]
        else:
            opening = (depth_weights, cot, gmb, saved[1][0], saved[1][2], left, right, y0, vectors[1])
            gyb, gx1, wide_sums, dots0, g1, be1, partial = mlp_backward(
                "first", opening, None, n2, u, act, 1, rw[2:], ew[2:], None
            )
            sums[0]["reduce_b"] = wide_sums[0]
            sums[1]["gain1"], sums[1]["shift1"] = wide_sums[8], wide_sums[16]
        g0, be0, left = mlp_backward(
            "own", None, gyb, n2, u, act, 0, rw[:2], ew[:2], partial
        )
        right = swap_core(left)
        shape_two = (2, 2 * units, half)
        mlp_total = reduce_grad(g0.reshape(shape_two), g1.reshape(shape_two), bits)
        opening = (gyb, left, right, mid, st2, vec)
        gmb, wide_sums, a1, db1, partial = attention_backward(
            opening, None, n1, aw[2:], cos, sin, segments, heads, 1, None
        )
        sums[l]["gain2"], sums[l]["shift2"], sums[l]["merge_b"] = (
            wide_sums[0],
            wide_sums[8],
            wide_sums[16],
        )
        a0, db0, left = attention_backward(
            None, gmb, n1, aw[:2], cos, sin, segments, heads, 0, partial
        )
        right = swap_core(left)
        attn_total = reduce_grad(a0, a1, bits)
        totals[l] = (mlp_total, attn_total)
        sums[l]["pair"] = ((db0[0], be0[0]), (db1[0], be1[0]))
    gx0, wide_sums = final_backward(gmb, saved[0][0], saved[0][2], left, right, vectors[0])
    sums[0]["gain1"], sums[0]["shift1"] = wide_sums[0], wide_sums[8]

    def quarter_of(value):
        return lambda index: lax.dynamic_slice_in_dim(value, index * part, part, 0)

    g0_home = from_row(quarter_of(gx1), row, core, flip)
    input_grad = from_row(quarter_of(gx0), row, core, flip)

    history_out = []
    for j in range(HISTORY):
        term = depth_weights[0, j] * g0_home
        if j >= 1:
            term = term + depth_weights[1, j - 1] * cotangent
        history_out.append(term)

    def by_core(value):
        return jnp.where(core == 0, jnp.sum(value), 0.0)

    mix0 = [jnp.sum(g0_home * history[j]) for j in range(HISTORY)] + [by_core(dots0[0])]
    mix1 = [jnp.sum(cotangent * history[j + 1]) for j in range(last)] + [
        by_core(dots1[0]),
        by_core(dots1[1]),
    ]
    mix_sum = jnp.concatenate([jnp.stack(mix0), jnp.stack(mix1)])
    mix_sum = mix_sum + swap_core(mix_sum)

    names = ("gain1", "shift1", "gain2", "shift2", "merge_b", "reduce_b")
    lines = []
    for index, which in ((2 * flip + core, 0), (2 * (1 - flip) + core, 1)):
        line = []
        for l in range(LAYERS):
            stacked = jnp.stack([sums[l][name] for name in names])
            cut = lax.dynamic_slice_in_dim(stacked, index * part, part, 1)
            line += [sums[l]["pair"][which][0], sums[l]["pair"][which][1], cut.reshape(-1)]
        lines.append(jnp.concatenate(line + [mix_sum]))
    total = lines[0] + swap_row(lines[1])
    for step in range(len(bits)):
        total = total + swap_dp(total, 1 << step)
    mix_grad = total[-mix_sum.shape[0] :].reshape(LAYERS, HISTORY + 1)
    per_layer = total[: -mix_sum.shape[0]].reshape(LAYERS, -1)
    wide_out = [per_layer[:, at + i * part : at + (i + 1) * part] for i in range(6)]

    attn_t, expand_t, reduce_t = [], [], []
    for l in range(LAYERS):
        (near, far), (attn_near, attn_far) = totals[l]
        attn_t.append(ordered(attn_near, attn_far, bit, 1))
        expand_t.append(ordered(near[:units], far[:units], bit, 1).T)
        reduce_t.append(ordered(near[units:], far[units:], bit, 1))
    attn_t = jnp.stack(attn_t).astype(F32)
    expand_t = jnp.stack(expand_t).astype(F32)
    reduce_t = jnp.stack(reduce_t).astype(F32)
    return (
        output,
        input_grad,
        jnp.stack(history_out),
        attn_t[:, : 3 * part].reshape(LAYERS, 3, part, width),
        per_layer[:, : 3 * part].reshape(LAYERS, 3, part),
        attn_t[:, 3 * part :],
        wide_out[4],
        wide_out[0],
        wide_out[1],
        wide_out[2],
        wide_out[3],
        expand_t,
        per_layer[:, 3 * part : at],
        reduce_t,
        wide_out[5],
        mix_grad,
    )


def solution(mesh):
    in_specs = (
        P("mp", "dp"),
        P(None, "mp", "dp"),
        P("dp", None),
        P("mp", "dp"),
        P(None, None, "mp", None),
        P(None, None, "mp"),
        P(None, "mp", None),
        P(None, "mp"),
        P(None, "mp"),
        P(None, "mp"),
        P(None, "mp"),
        P(None, "mp"),
        P(None, None, "mp"),
        P(None, "mp"),
        P(None, "mp", None),
        P(None, "mp"),
        P(),
    )
    out_specs = (
        P("mp", "dp"),
        P("mp", "dp"),
        P(None, "mp", "dp"),
        P(None, None, "mp", None),
        P(None, None, "mp"),
        P(None, "mp", None),
        P(None, "mp"),
        P(None, "mp"),
        P(None, "mp"),
        P(None, "mp"),
        P(None, "mp"),
        P(None, None, "mp"),
        P(None, "mp"),
        P(None, "mp", None),
        P(None, "mp"),
        P(),
    )
    return jax.shard_map(shards, mesh=mesh, in_specs=in_specs, out_specs=out_specs, check_vma=False)
```

```python
import functools

import jax
import jax.numpy as jnp
from jax import lax
from jax.experimental import pallas as pl
from jax.experimental.pallas import tpu as pltpu
from jax.sharding import PartitionSpec as P

HEAD = 64
HALF = HEAD // 2
LAYERS = 2
HISTORY = 4
EPS = 1e-05
MASKED = -1e30
BLK = 256
REACH = 512
TILE = 256
STRIP = 96
BF = jnp.bfloat16
F32 = jnp.float32
GELU_A = 0.7978845608028654
GELU_B = 0.044715
GAIN1, SHIFT1, GAIN2, SHIFT2, MERGE_B, REDUCE_B, INPUT_B, EXPAND_B = 0, 1, 2, 3, 4, 5, 6, 8


def dot(a, b, on):
    return lax.dot_general(a, b, (on, ((), ())), preferred_element_type=F32)


def nn(a, b):
    return dot(a, b, ((1,), (0,)))


def nt(a, b):
    return dot(a, b, ((1,), (1,)))


def tn(a, b):
    return dot(a, b, ((0,), (0,)))


def full(shape):
    return pl.BlockSpec(shape, lambda t: (0,) * len(shape))


def shape(dims, kind=BF):
    return jax.ShapeDtypeStruct(dims, kind)


def launch(kernel, name, steps, ins, outs, scratch, micros, vmem, aliases=None):
    return pl.pallas_call(
        kernel,
        grid=(steps,),
        in_specs=[spec for _, spec in ins],
        out_specs=[spec for _, spec in outs],
        out_shape=[struct for struct, _ in outs],
        scratch_shapes=scratch,
        compiler_params=pltpu.CompilerParams(
            dimension_semantics=("arbitrary",), vmem_limit_bytes=vmem * 1024 * 1024
        ),
        cost_estimate=pl.CostEstimate(
            flops=int(micros * 1.0e9), bytes_accessed=1 << 20, transcendentals=0
        ),
        input_output_aliases=aliases or {},
        name=name,
    )(*[operand for operand, _ in ins])


def whole(*operands):
    return [(operand, full(operand.shape)) for operand in operands]


def scalars(operand):
    return [(operand, pl.BlockSpec(memory_space=pltpu.SMEM))]


def out_full(dims, kind=BF):
    return (shape(dims, kind), full(dims))


class Pieces:
    def __init__(self, refs):
        self.refs = refs
        self.size = refs[0].shape[0]

    def __getitem__(self, index):
        rows = index[0]
        at = rows.start // self.size
        return self.refs[at][slice(rows.start - at * self.size, rows.stop - at * self.size), :]

    def store(self, at, value):
        for start in range(0, value.shape[0], self.size):
            self.refs[(at + start) // self.size][...] = value[start : start + self.size].astype(BF)


def out_pieces(width, length):
    return [out_full((width // 4, length)) for _ in range(4)]


def strips(size):
    return [slice(at, at + STRIP) for at in range(0, size, STRIP)]


def key_range(block):
    return max(0, block * BLK - REACH), (block + 1) * BLK


def mask_shape(length):
    return (length // BLK, min(length, REACH + BLK), BLK)


def fill_mask(mask, segments, length):
    line = segments[...]
    column = jnp.broadcast_to(line, (8, length)).T[:, 0:1]
    for block in range(length // BLK):
        low, high = key_range(block)
        span = high - low
        here = line[:, block * BLK : high]
        there = column[low:high, :]
        query_pos = lax.broadcasted_iota(jnp.int32, (span, BLK), 1) + block * BLK
        key_pos = lax.broadcasted_iota(jnp.int32, (span, BLK), 0) + low
        allowed = (here == there) & (key_pos <= query_pos)
        mask[block, :span, :] = jnp.where(allowed, 0.0, MASKED)


def normalise(source, target, stats, columns, gain, shift, width, length):
    total = jnp.zeros((1, length), F32)
    squares = jnp.zeros((1, length), F32)
    for rows in strips(width):
        x = source(rows)
        total += jnp.sum(x, 0, keepdims=True)
        squares += jnp.sum(x * x, 0, keepdims=True)
    mean = total * (1.0 / width)
    scale = lax.rsqrt(squares * (1.0 / width) - mean * mean + EPS)
    stats[0:1, :] = mean
    stats[1:2, :] = scale
    return mean, scale


def apply_norm(x, mean, scale, columns, gain, shift, rows):
    return ((x - mean) * scale * columns[rows, gain : gain + 1] + columns[rows, shift : shift + 1]).astype(BF)


def norm_back(x, stats, left, right, base, gain, width, length, grad_n, grad_gain, emit):
    mean, scale = stats[0:1, :], stats[1:2, :]
    first = jnp.zeros((1, length), F32)
    second = jnp.zeros((1, length), F32)
    for rows in strips(width):
        hat = (x[rows, :].astype(F32) - mean) * scale
        grad = left[rows, :].astype(F32) + right[rows, :].astype(F32)
        grad_n[rows, :] = grad.astype(BF)
        product = grad * hat
        grad_gain[rows, :] = product.astype(BF)
        column = gain[rows]
        first += jnp.sum(grad * column, 0, keepdims=True)
        second += jnp.sum(product * column, 0, keepdims=True)
    first = first * (1.0 / width)
    second = second * (1.0 / width)
    for rows in strips(width):
        hat = (x[rows, :].astype(F32) - mean) * scale
        grad = left[rows, :].astype(F32) + right[rows, :].astype(F32)
        emit(rows, base(rows) + scale * (grad * gain[rows] - first - hat * second))


def row_sums(value):
    return nt(jnp.ones((8, value.shape[1]), BF), value)


def attention_forward_kernel(mixing, heads, length, width, *refs):
    refs = list(refs)
    if mixing:
        coef, history_i, mid_i = refs[:3]
        left, right, before = Pieces(refs[3:7]), Pieces(refs[7:11]), refs[11]
        del refs[:12]
    else:
        x_i = refs.pop(0)
    vectors, a0d, a0r, a1d, a1r, cos, sin, segments = refs[:8]
    del refs[:8]
    if mixing:
        y_o, x_o = refs[:2]
        del refs[:2]
    n1_o, st_o, q_o, k_o, v_o, o_o, lse_o = refs[:7]
    part_o = Pieces(refs[7:11])
    lin, mask, o_all = refs[11:]
    head = pl.program_id(0)
    quarter = (heads // 2) * HEAD
    half = width // 2

    @pl.when(head == 0)
    def _():
        columns = vectors[...].T
        if mixing:
            bias = before[...].T
            weight = coef[0, HISTORY]
            for rows in strips(width):
                y = (
                    mid_i[rows, :].astype(F32)
                    + left[rows, :].astype(F32)
                    + right[rows, :].astype(F32)
                    + bias[rows, REDUCE_B : REDUCE_B + 1]
                )
                y_o[rows, :] = y.astype(BF)
                x_o[rows, :] = (history_i[rows, :].astype(F32) + weight * y).astype(BF)
            source = x_o
        else:
            source = x_i
        mean, scale = normalise(
            lambda rows: source[rows, :].astype(F32), None, st_o, None, None, None, width, length
        )
        for rows in strips(width):
            n1_o[rows, :] = apply_norm(
                source[rows, :].astype(F32), mean, scale, columns, GAIN1, SHIFT1, rows
            )
        for index, (d, r) in enumerate(((a0d, a0r), (a1d, a1r))):
            at = index * 3 * quarter
            lin[at : at + 3 * quarter, :] = (
                nn(d[: 3 * quarter, :], n1_o[:half, :])
                + nn(r[: 3 * quarter, :], n1_o[half:, :])
                + columns[: 3 * quarter, INPUT_B + index : INPUT_B + index + 1]
            )
        fill_mask(mask, segments, length)

    c, s = cos[...], sin[...]
    group = head // (heads // 2)
    base = group * 3 * quarter + (head - group * (heads // 2)) * HEAD

    def rope(start):
        first = lin[pl.ds(pl.multiple_of(start, HALF), HALF), :]
        second = lin[pl.ds(pl.multiple_of(start + HALF, HALF), HALF), :]
        return jnp.concatenate([first * c - second * s, second * c + first * s], 0)

    q = (rope(base).astype(BF) * BF(HEAD**-0.5)).astype(BF)
    key = rope(base + quarter).astype(BF)
    v = lin[pl.ds(pl.multiple_of(base + 2 * quarter, HEAD), HEAD), :].astype(BF)
    q_o[0] = q
    k_o[0] = key
    v_o[0] = v
    for block in range(length // BLK):
        low, high = key_range(block)
        cols = slice(block * BLK, high)
        scores = tn(key[:, low:high], q[:, cols]) + mask[block, : high - low, :]
        peak = jnp.max(scores, 0, keepdims=True)
        weights = jnp.exp(scores - peak)
        total = jnp.sum(weights, 0, keepdims=True)
        out = (nn(v[:, low:high], weights.astype(BF)) * (1.0 / total)).astype(BF)
        o_o[0, :, cols] = out
        o_all[pl.ds(pl.multiple_of(head * HEAD, HEAD), HEAD), cols] = out
        lse_o[0, :, cols] = peak + jnp.log(total)

    @pl.when(head == heads - 1)
    def _():
        for at, own, other in ((0, a0d, a1d), (half, a0r, a1r)):
            part_o.store(
                at,
                tn(own[3 * quarter :, :], o_all[:quarter, :])
                + tn(other[3 * quarter :, :], o_all[quarter:, :]),
            )


def attention_forward(mix, x, vectors, weights, cos, sin, segments):
    length = segments.shape[1]
    rows, half = weights[0].shape
    width = 2 * half
    quarter = rows // 4
    heads = 2 * quarter // HEAD
    if mix is not None:
        ins = scalars(mix[0]) + whole(*mix[1:])
        outs = [out_full((width, length)), out_full((width, length))]
    else:
        ins = whole(x)
        outs = []
    ins = ins + whole(vectors, *weights, cos, sin, segments)
    per_head = lambda size: pl.BlockSpec((1, size, length), lambda h: (h, 0, 0))
    heads_out = (shape((heads, HEAD, length)), per_head(HEAD))
    outs = outs + [
        out_full((width, length)),
        out_full((8, length), F32),
        heads_out,
        heads_out,
        heads_out,
        heads_out,
        (shape((heads, 1, length), F32), per_head(1)),
    ]
    outs = outs + out_pieces(width, length)
    return launch(
        functools.partial(attention_forward_kernel, mix is not None, heads, length, width),
        "attention_forward",
        heads,
        ins,
        outs,
        [
            pltpu.VMEM((6 * quarter, length), F32),
            pltpu.VMEM(mask_shape(length), F32),
            pltpu.VMEM((2 * quarter, length), BF),
        ],
        20,
        44,
    )


def halves_of(refs, natural, place, half):
    if not natural:
        return [lambda index, value, ref=ref: ref.__setitem__(index, value.astype(BF)) for ref in refs]

    def at(which):
        cols = pl.ds(pl.multiple_of((place[0, 0] ^ which) * half, half), half)

        def put(index, value):
            refs[0][index[:-1] + (cols,)] = value.astype(BF)

        return put

    return [at(0), at(1)]


def attention_backward_kernel(opening, natural, heads, length, width, *refs):
    refs = list(refs)
    place = refs.pop(0)
    if opening:
        grad_i, mid, st, vectors = refs[0], refs[9], refs[10], refs[11]
        left, right = Pieces(refs[1:5]), Pieces(refs[5:9])
        del refs[:12]
    else:
        gmb = refs.pop(0)
    n1, ad, ar, cos, sin, segments, q_i, k_i, v_i, o_i, lse_i = refs[:11]
    del refs[:11]
    if opening:
        gmb, sums_o = refs[:2]
        del refs[:2]
    else:
        add = refs.pop(0)
    count = 1 if natural else 2
    put = halves_of(refs[:count], natural, place, width // 2)
    db_o = refs[count]
    del refs[: count + 1]
    if opening:
        part_o = refs.pop(0)
    else:
        part_o = Pieces(refs[:4])
        del refs[:4]
    mask, go_all, gl_all, gk_s, gv_s = refs[:5]
    del refs[:5]
    head = pl.program_id(0)
    quarter = heads * HEAD
    half = width // 2

    @pl.when(head == 0)
    def _():
        if opening:
            grad_n, grad_gain = refs
            columns = vectors[...].T
            norm_back(
                mid,
                st,
                left,
                right,
                lambda rows: grad_i[rows, :].astype(F32),
                columns[:, GAIN2 : GAIN2 + 1],
                width,
                length,
                grad_n,
                grad_gain,
                lambda rows, value: gmb.__setitem__((rows, slice(None)), value.astype(BF)),
            )
            sums_o[0:8, :] = row_sums(grad_gain[...])
            sums_o[8:16, :] = row_sums(grad_n[...])
            sums_o[16:24, :] = row_sums(gmb[...])
        go_all[...] = (
            nn(ad[3 * quarter :, :], gmb[:half, :]) + nn(ar[3 * quarter :, :], gmb[half:, :])
        ).astype(BF)
        o_flat = o_i[...].reshape(quarter, length)
        below = (slice(3 * quarter, 4 * quarter), slice(None))
        put[0](below, nt(o_flat, gmb[:half, :]))
        put[1](below, nt(o_flat, gmb[half:, :]))
        fill_mask(mask, segments, length)

    base = pl.multiple_of(head * HEAD, HEAD)
    q, key, v = q_i[0], k_i[0], v_i[0]
    go = go_all[pl.ds(base, HEAD), :]
    delta = jnp.sum(go.astype(F32) * o_i[head].astype(F32), 0, keepdims=True)
    gk_s[...] = jnp.zeros_like(gk_s)
    gv_s[...] = jnp.zeros_like(gv_s)
    gq_parts = []
    for block in range(length // BLK):
        low, high = key_range(block)
        cols = slice(block * BLK, high)
        scores = tn(key[:, low:high], q[:, cols]) + mask[block, : high - low, :]
        probs = jnp.exp(scores - lse_i[0, :, cols])
        grad_probs = tn(v[:, low:high], go[:, cols])
        grad_scores = (probs * (grad_probs - delta[:, cols])).astype(BF)
        gv_s[:, low:high] += nt(go[:, cols], probs.astype(BF))
        gk_s[:, low:high] += nt(q[:, cols], grad_scores)
        gq_parts.append(nn(key[:, low:high], grad_scores))
    c, s = cos[...], sin[...]

    def store(part, top, bottom):
        start = pl.multiple_of(part * quarter + base, HEAD)
        gl_all[pl.ds(start, HEAD), :] = jnp.concatenate([top, bottom], 0).astype(BF)

    gq = jnp.concatenate(gq_parts, 1) * HEAD**-0.5
    store(0, gq[:HALF] * c + gq[HALF:] * s, gq[HALF:] * c - gq[:HALF] * s)
    gk = gk_s[...]
    store(1, gk[:HALF] * c + gk[HALF:] * s, gk[HALF:] * c - gk[:HALF] * s)
    store(2, gv_s[:HALF, :], gv_s[HALF:, :])

    @pl.when(head == heads - 1)
    def _():
        db_o[...] = row_sums(gl_all[...])
        above = (slice(0, 3 * quarter), slice(None))
        put[0](above, nt(gl_all[...], n1[:half, :]))
        put[1](above, nt(gl_all[...], n1[half:, :]))
        for at, w in ((0, ad), (half, ar)):
            value = tn(w[: 3 * quarter, :], gl_all[...])
            if opening:
                part_o[at : at + half, :] = value
            else:
                part_o.store(at, value + add[at : at + half, :])


def attention_backward(place, natural, opening, gmb, n1, weights, cos, sin, segments, saved, group, add):
    length = segments.shape[1]
    rows, half = weights[0].shape
    width = 2 * half
    quarter = rows // 4
    heads = quarter // HEAD
    q, key, v, o, lse = saved
    if opening is not None:
        ins = scalars(place) + whole(*opening)
        outs = [out_full((width, length)), out_full((24, width), F32)]
        scratch = [pltpu.VMEM((width, length), BF), pltpu.VMEM((width, length), BF)]
    else:
        ins = scalars(place) + whole(gmb)
        outs = []
        scratch = []
    at = group * heads
    per_head = lambda size: pl.BlockSpec((1, size, length), lambda h: (at + h, 0, 0))
    ins = ins + whole(n1, *weights, cos, sin, segments)
    ins = ins + [(item, per_head(HEAD)) for item in (q, key, v)]
    ins = ins + [(o, pl.BlockSpec((heads, HEAD, length), lambda h: (group, 0, 0))), (lse, per_head(1))]
    if add is not None:
        ins = ins + whole(add)
    outs = outs + ([out_full((rows, width))] if natural else [out_full((rows, half))] * 2)
    outs = outs + [out_full((8, 3 * quarter), F32)]
    outs = outs + (out_pieces(width, length) if add is not None else [out_full((width, length), F32)])
    return launch(
        functools.partial(
            attention_backward_kernel, opening is not None, natural, heads, length, width
        ),
        "attention_backward",
        heads,
        ins,
        outs,
        [
            pltpu.VMEM(mask_shape(length), F32),
            pltpu.VMEM((quarter, length), BF),
            pltpu.VMEM((3 * quarter, length), BF),
            pltpu.VMEM((HEAD, length), F32),
            pltpu.VMEM((HEAD, length), F32),
        ]
        + scratch,
        14,
        44,
    )


def mlp_forward_kernel(merged, tiles, length, width, *refs):
    refs = list(refs)
    x, left, right, vectors = refs[0], Pieces(refs[1:5]), Pieces(refs[5:9]), refs[9]
    e0d, e0r, e1d, e1r = refs[10:14]
    del refs[:14]
    if merged:
        r0d, r0r, r1d, r1r = refs[:4]
        del refs[:4]
    mid_o, n2_o, st_o, u_o, act_o = refs[:5]
    del refs[:5]
    columns_s = refs.pop(0 if not merged else 4)
    if merged:
        part_o, acts = Pieces(refs[:4]), refs[4]
    t = pl.program_id(0)
    half = width // 2
    units = tiles * TILE

    @pl.when(t == 0)
    def _():
        columns = vectors[...].T
        columns_s[:, : columns.shape[1]] = columns
        for rows in strips(width):
            mid_o[rows, :] = (
                x[rows, :].astype(F32)
                + left[rows, :].astype(F32)
                + right[rows, :].astype(F32)
                + columns[rows, MERGE_B : MERGE_B + 1]
            ).astype(BF)
        mean, scale = normalise(
            lambda rows: mid_o[rows, :].astype(F32), None, st_o, None, None, None, width, length
        )
        for rows in strips(width):
            n2_o[rows, :] = apply_norm(
                mid_o[rows, :].astype(F32), mean, scale, columns, GAIN2, SHIFT2, rows
            )

    def expand(group, d, r):
        at = pl.multiple_of((t - group * tiles) * TILE, TILE)
        bias = columns_s[pl.ds(at, TILE), EXPAND_B + group : EXPAND_B + group + 1]
        u = tn(d[...], n2_o[:half, :]) + tn(r[...], n2_o[half:, :]) + bias
        act = (0.5 * u * (1.0 + jnp.tanh(GELU_A * (u + GELU_B * (u * u * u))))).astype(BF)
        u_o[...] = u.astype(BF)
        act_o[...] = act
        if merged:
            acts[pl.ds(pl.multiple_of(t * TILE, TILE), TILE), :] = act

    @pl.when(t < tiles)
    def _():
        expand(0, e0d, e0r)

    @pl.when(t >= tiles)
    def _():
        expand(1, e1d, e1r)

    if merged:

        @pl.when(t == 2 * tiles - 1)
        def _():
            for at, own, other in ((0, r0d, r1d), (half, r0r, r1r)):
                part_o.store(at, tn(own[...], acts[:units, :]) + tn(other[...], acts[units:, :]))


def mlp_forward(x, left, right, vectors, expand, reduce):
    width, length = x.shape
    half, units = expand[0].shape
    tiles = units // TILE
    merged = reduce is not None
    first = pl.BlockSpec((half, TILE), lambda t: (0, jnp.minimum(t, tiles - 1)))
    second = pl.BlockSpec((half, TILE), lambda t: (0, jnp.maximum(t - tiles, 0)))
    ins = whole(x, *left, *right, vectors)
    ins = ins + list(zip(expand, (first, first, second, second)))
    per_tile = (shape((2 * units, length)), pl.BlockSpec((TILE, length), lambda t: (t, 0)))
    outs = [
        out_full((width, length)),
        out_full((width, length)),
        out_full((8, length), F32),
        per_tile,
        per_tile,
    ]
    scratch = [pltpu.VMEM((width, 128), F32)]
    if merged:
        ins = ins + whole(*reduce)
        outs = outs + out_pieces(width, length)
        scratch = scratch + [pltpu.VMEM((2 * units, length), BF)]
    return launch(
        functools.partial(mlp_forward_kernel, merged, tiles, length, width),
        "mlp_forward",
        2 * tiles,
        ins,
        outs,
        scratch,
        14 if merged else 10,
        44,
    )


def reduce_forward_kernel(units, half, act, *refs):
    r0d, r0r, r1d, r1r = refs[:4]
    part_o = Pieces(refs[4:])
    for at, own, other in ((0, r0d, r1d), (half, r0r, r1r)):
        part_o.store(at, tn(own[...], act[:units, :]) + tn(other[...], act[units:, :]))


def reduce_forward(act, reduce):
    units, half = reduce[0].shape
    length = act.shape[1]
    return launch(
        functools.partial(reduce_forward_kernel, units, half),
        "reduce_forward",
        1,
        whole(act, *reduce),
        out_pieces(2 * half, length),
        [],
        4,
        32,
    )


def mlp_backward_kernel(mode, natural, tiles, length, width, *refs):
    refs = list(refs)
    place = refs.pop(0)
    half = width // 2
    units = tiles * TILE
    if mode == "last":
        coef, cot, mid = refs[:3]
        left, right = Pieces(refs[3:7]), Pieces(refs[7:11])
        y0, vectors = refs[11:13]
        del refs[:13]
    elif mode == "first":
        coef, cot, gmid, x, st = refs[:5]
        left, right = Pieces(refs[5:9]), Pieces(refs[9:13])
        y0, vectors = refs[13:15]
        del refs[:15]
    else:
        gyb = refs.pop(0)
    n2, u_i, act, rd, rr, ed, er = refs[:7]
    del refs[:7]
    if mode == "own":
        add = refs.pop(0)
    else:
        gyb = refs.pop(0)
        if mode == "first":
            gx_o = refs.pop(0)
        sums_o, dots_o = refs[:2]
        del refs[:2]
    count = 1 if natural else 2
    put_expand = halves_of(refs[:count], natural, place, half)
    put_reduce = halves_of(refs[count : 2 * count], natural, place, half)
    be_o = refs[2 * count]
    del refs[: 2 * count + 1]
    if mode == "own":
        part_o = Pieces(refs[:4])
        del refs[:4]
    else:
        part_o = refs.pop(0)
    gubs = refs.pop(0)
    t = pl.program_id(0)

    if mode != "own":

        @pl.when(t == 0)
        def _():
            columns = vectors[...].T
            dots_o[...] = jnp.zeros_like(dots_o)
            if mode == "last":
                for rows in strips(width):
                    value = cot[rows, :].astype(F32)
                    gyb[rows, :] = (coef[1, HISTORY] * value).astype(BF)
                    y1 = (
                        mid[rows, :].astype(F32)
                        + left[rows, :].astype(F32)
                        + right[rows, :].astype(F32)
                        + columns[rows, REDUCE_B : REDUCE_B + 1]
                    )
                    dots_o[0:1, :] += jnp.sum(value * y0[rows, :].astype(F32), 0, keepdims=True)
                    dots_o[1:2, :] += jnp.sum(value * y1, 0, keepdims=True)
                sums_o[0:8, :] = row_sums(gyb[...])
            else:
                grad_n, grad_gain = refs

                def emit(rows, value):
                    gx_o[rows, :] = value.astype(BF)
                    gyb[rows, :] = (
                        coef[1, HISTORY - 1] * cot[rows, :].astype(F32) + coef[0, HISTORY] * value
                    ).astype(BF)
                    dots_o[0:1, :] += jnp.sum(value * y0[rows, :].astype(F32), 0, keepdims=True)

                norm_back(
                    x,
                    st,
                    left,
                    right,
                    lambda rows: gmid[rows, :].astype(F32),
                    columns[:, GAIN1 : GAIN1 + 1],
                    width,
                    length,
                    grad_n,
                    grad_gain,
                    emit,
                )
                sums_o[0:8, :] = row_sums(gyb[...])
                sums_o[8:16, :] = row_sums(grad_gain[...])
                sums_o[16:24, :] = row_sums(grad_n[...])

    ga = nn(rd[...], gyb[:half, :]) + nn(rr[...], gyb[half:, :])
    u = u_i[...].astype(F32)
    square = u * u
    th = jnp.tanh(GELU_A * u * (1.0 + GELU_B * square))
    slope = 0.5 * (1.0 + th) + (0.5 * GELU_A) * u * (1.0 - th * th) * (1.0 + (3.0 * GELU_B) * square)
    gub = (ga * slope).astype(BF)
    gubs[pl.ds(pl.multiple_of(t * TILE, TILE), TILE), :] = gub
    be_o[...] = row_sums(gub)
    every = (slice(None), slice(None))
    for index, rows in enumerate((slice(0, half), slice(half, width))):
        put_expand[index](every, nt(gub, n2[rows, :]))
        put_reduce[index](every, nt(act[...], gyb[rows, :]))

    @pl.when(t == tiles - 1)
    def _():
        for at, w in ((0, ed), (half, er)):
            value = nn(w[...], gubs[...])
            if mode == "own":
                part_o.store(at, value + add[at : at + half, :])
            else:
                part_o[at : at + half, :] = value


def mlp_backward(place, natural, mode, opening, gyb, n2, u, act, group, reduce, expand, add):
    width, length = n2.shape
    half, units = expand[0].shape
    tiles = units // TILE
    outs = []
    scratch = [pltpu.VMEM((units, length), BF)]
    if mode == "own":
        ins = scalars(place) + whole(gyb)
    else:
        ins = scalars(place) + scalars(opening[0]) + whole(*opening[1:])
        outs = outs + [out_full((width, length))]
        if mode == "first":
            outs = outs + [out_full((width, length))]
            scratch = scratch + [pltpu.VMEM((width, length), BF), pltpu.VMEM((width, length), BF)]
        outs = outs + [out_full((24, width), F32), out_full((8, length), F32)]
    at = group * tiles
    per_tile = pl.BlockSpec((TILE, length), lambda t: (at + t, 0))
    reduce_tile = pl.BlockSpec((TILE, half), lambda t: (t, 0))
    ins = ins + whole(n2) + [(u, per_tile), (act, per_tile)]
    ins = ins + [(item, reduce_tile) for item in reduce] + whole(*expand)
    if add is not None:
        ins = ins + whole(add)
    if natural:
        outs = outs + [(shape((units, width)), pl.BlockSpec((TILE, width), lambda t: (t, 0)))] * 2
    else:
        outs = outs + [(shape((units, half)), reduce_tile)] * 4
    outs = outs + [
        (shape((8, units), F32), pl.BlockSpec((8, TILE), lambda t: (0, t))),
    ]
    outs = outs + (out_pieces(width, length) if add is not None else [out_full((width, length), F32)])
    return launch(
        functools.partial(mlp_backward_kernel, mode, natural, tiles, length, width),
        "mlp_backward",
        tiles,
        ins,
        outs,
        scratch,
        13,
        44,
    )


def final_kernel(length, width, *refs):
    gmid, x, st = refs[:3]
    left, right = Pieces(refs[3:7]), Pieces(refs[7:11])
    vectors, gx_o, sums_o, grad_n, grad_gain = refs[11:]
    columns = vectors[...].T
    norm_back(
        x,
        st,
        left,
        right,
        lambda rows: gmid[rows, :].astype(F32),
        columns[:, GAIN1 : GAIN1 + 1],
        width,
        length,
        grad_n,
        grad_gain,
        lambda rows, value: gx_o.__setitem__((rows, slice(None)), value.astype(BF)),
    )
    sums_o[0:8, :] = row_sums(grad_gain[...])
    sums_o[8:16, :] = row_sums(grad_n[...])


def final_backward(*operands):
    width, length = operands[0].shape
    return launch(
        functools.partial(final_kernel, length, width),
        "norm_backward",
        1,
        whole(*operands),
        [out_full((width, length)), out_full((16, width), F32)],
        [pltpu.VMEM((width, length), BF), pltpu.VMEM((width, length), BF)],
        5,
        32,
    )


def swap_core(value):
    size = lax.axis_size("mp")
    return lax.ppermute(value, "mp", [(i, i ^ 1) for i in range(size)])


def swap_row(value):
    size = lax.axis_size("mp")
    return lax.ppermute(value, "mp", [(i, i ^ 2) for i in range(size)])


def swap_dp(value, bit):
    size = lax.axis_size("dp")
    return lax.ppermute(value, "dp", [(i, i ^ bit) for i in range(size)])


def half_of(value, which, axis=0):
    size = value.shape[axis] // 2
    return lax.dynamic_slice_in_dim(value, which * size, size, axis)


def ordered(mine, theirs, which, axis=0):
    return jnp.where(
        which == 0,
        jnp.concatenate([mine, theirs], axis),
        jnp.concatenate([theirs, mine], axis),
    )


def spread(mine, flip, core):
    theirs = swap_row(mine)
    pair = ordered(mine[None], theirs[None], flip)
    other = swap_core(pair)
    return (
        jnp.where(
            core == 0,
            jnp.stack([pair[0], other[0], pair[1], other[1]]),
            jnp.stack([other[0], pair[0], other[1], pair[1]]),
        ),
        theirs,
    )


def row_steps(value, row, core, flip):
    length = value.shape[1] // 2
    low = value.astype(BF)
    mine = lax.dynamic_slice_in_dim(low, row * length, length, 1)
    (theirs,) = yield [swap_row(lax.dynamic_slice_in_dim(low, (1 - row) * length, length, 1))]
    pair = ordered(mine[None], theirs[None], flip)
    other = swap_core(pair)
    gathered = jnp.where(
        core == 0,
        jnp.stack([pair[0], other[0], pair[1], other[1]]),
        jnp.stack([other[0], pair[0], other[1], pair[1]]),
    )
    yield gathered.reshape(4 * value.shape[0], length)


def home_steps(mine, sent, row):
    (theirs,) = yield [swap_row(sent)]
    yield ordered(mine, theirs, row, 1).astype(F32)


def fetch_steps(near, far, relay):
    (direct,) = yield [swap_row(near)]
    (rest,) = yield [swap_dp(direct, 1) if relay else swap_row(far)]
    yield direct, rest


class Weight:
    def __init__(self, near, far, relay=True):
        self.own = (near, far)
        self.chain = Chain(fetch_steps(near, far, relay))

    def other(self):
        return self.chain.finish()

    def parts(self):
        return self.own + tuple(self.other())


def swap_pieces(pieces):
    return [swap_core(piece) for piece in pieces]


def add_kernel(count, *refs):
    for a, b, out in zip(refs[:count], refs[count : 2 * count], refs[2 * count :]):
        out[...] = (a[...].astype(F32) + b[...].astype(F32)).astype(BF)


def add_all(mine, theirs):
    return launch(
        functools.partial(add_kernel, len(mine)),
        "add",
        1,
        whole(*mine, *theirs),
        [out_full(item.shape) for item in mine],
        [],
        2,
        16,
    )


def add_low(mine, theirs):
    return (mine.astype(F32) + theirs.astype(F32)).astype(BF)


def assemble_kernel(turned, counts, halves, *refs):
    if halves:
        place, near, far = refs[:3]
        scratch = refs[-1]
        outs = refs[len(refs) - 1 - len(counts) : -1]
        half = near.shape[1]
        a, b = near[...].astype(F32), far[...].astype(F32)
        first = place[0, 0] == 0
        scratch[:, :half] = jnp.where(first, a, b)
        scratch[:, half:] = jnp.where(first, b, a)
    else:
        scratch = refs[0]
        outs = refs[len(refs) - len(counts) :]
    at = 0
    for out, count in zip(outs, counts):
        value = scratch[at : at + count, :].astype(F32)
        out[...] = (value.T if turned else value).reshape(out.shape)
        at += count


def assemble(total, place, layer, shapes, counts, turned, held):
    halves = isinstance(total, tuple)
    ins = scalars(place) + whole(*total) if halves else whole(total)
    aliases = {}
    if held is not None:
        for index, item in enumerate(held):
            aliases[len(ins)] = index
            ins.append((item, pl.BlockSpec(memory_space=pl.ANY)))
    outs = []
    for dims in shapes:
        block = pl.BlockSpec((1,) + dims[1:], lambda t, dims=dims: (layer,) + (0,) * (len(dims) - 1))
        outs.append((shape(dims, F32), block))
    rows = sum(counts)
    scratch = [pltpu.VMEM((rows, 2 * total[0].shape[1]), F32)] if halves else []
    return launch(
        functools.partial(assemble_kernel, turned, counts, halves),
        "assemble",
        1,
        ins,
        outs,
        scratch,
        3,
        24,
        aliases,
    )


def reduce_steps(own, other, bits):
    (near,) = yield [swap_row(other[0])]
    near, far = yield [near, swap_row(other[1])]
    near, far = add_all(own, (near, far))
    got = yield [swap_dp(far, 1)]
    (value,) = add_all((near,), got)
    for step in range(1, len(bits)):
        away = half_of(value, 1 - bits[step])
        got = yield [swap_dp(away, 1 << step)]
        value = add_low(half_of(value, bits[step]), got[0])
    for step in reversed(range(1, len(bits))):
        got = yield [swap_dp(value, 1 << step)]
        value = ordered(value, got[0], bits[step])
    got = yield [swap_dp(value, 1)]
    yield value, got[0]


def whole_steps(own, other):
    (got,) = yield [swap_row(other)]
    yield add_all((own,), (got,))


class Chain:
    def __init__(self, steps):
        self.steps = steps
        self.held = None

    def advance(self):
        try:
            self.held = self.steps.send(self.held)
            return True
        except StopIteration:
            return False

    def finish(self):
        while self.advance():
            pass
        return self.held


def pin(anchor, *chains):
    for chain in chains:
        chain.advance()
    held = lax.optimization_barrier((anchor, [chain.held for chain in chains]))
    for chain, value in zip(chains, held[1]):
        chain.held = value
    return held[0]


def shards(
    inputs,
    history,
    segment_ids,
    cotangent,
    input_weight,
    input_bias,
    merge_weight,
    merge_bias,
    first_gain,
    first_shift,
    second_gain,
    second_shift,
    expand_weight,
    expand_bias,
    reduce_weight,
    reduce_bias,
    depth_weights,
):
    member = lax.axis_index("mp")
    row, core = member // 2, member % 2
    dp = lax.axis_index("dp")
    bits = []
    size = lax.axis_size("dp")
    while (1 << len(bits)) < size:
        bits.append((dp >> len(bits)) & 1)
    bit = bits[0]
    flip = row ^ bit
    length = segment_ids.shape[1]
    part = inputs.shape[0]
    width = 4 * part
    half = width // 2
    units = expand_bias.shape[1]
    last = HISTORY - 1

    segments = lax.dynamic_slice_in_dim(segment_ids, row, 1, 0).astype(F32)
    frequency = 10000.0 ** (-jnp.arange(HALF, dtype=F32) * 2.0 / HEAD)
    angles = frequency[:, None] * jnp.arange(length, dtype=F32)[None, :]
    cos, sin = jnp.cos(angles), jnp.sin(angles)

    place = bit.reshape(1, 1).astype(jnp.int32)
    x0_chain = Chain(row_steps(inputs, row, core, flip))
    x0_chain.advance()

    small = jnp.concatenate(
        [
            item.reshape(LAYERS, -1)
            for item in (
                input_bias,
                expand_bias,
                first_gain,
                first_shift,
                second_gain,
                second_shift,
                merge_bias,
                reduce_bias,
            )
        ],
        1,
    )
    def low_halves(source, axis):
        return half_of(source, bit, axis).astype(BF), half_of(source, 1 - bit, axis).astype(BF)

    def merged(l, first, second):
        return jnp.concatenate([first[l].reshape(3 * part, width), second[l]], 0)

    attn_w = [Weight(*low_halves(merged(0, input_weight, merge_weight), 1))]
    attn_w[0].chain.advance()
    attn_w[0].chain.held, early, small = lax.optimization_barrier(
        (attn_w[0].chain.held, (expand_weight, reduce_weight), small)
    )
    expand_w = [Weight(*low_halves(early[0][0], 0))]
    expand_w[0].chain.advance()
    reduce_w = [Weight(*low_halves(early[1][0], 1))]
    quarters, small_other = spread(small, flip, core)
    at = 3 * part + units
    wide = quarters[:, :, at:].reshape(4, LAYERS, 6, part).transpose(1, 2, 0, 3)
    wide = wide.reshape(LAYERS, 6, width)
    pair = jnp.stack([small, small_other], 1)
    input_rows = jnp.pad(pair[:, :, : 3 * part], ((0, 0), (0, 0), (0, width - 3 * part)))
    vectors = jnp.concatenate(
        [wide, input_rows, pair[:, :, 3 * part : at], jnp.zeros((LAYERS, 6, width), F32)], 1
    )

    x0 = x0_chain.finish()
    x0, late_weights, past = lax.optimization_barrier(
        (x0, (input_weight, merge_weight, expand_weight, reduce_weight), history)
    )
    attn_w.append(Weight(*low_halves(merged(1, *late_weights[:2]), 1)))
    expand_w.append(Weight(*low_halves(late_weights[2][1], 0)))
    reduce_w.append(Weight(*low_halves(late_weights[3][1], 1), relay=False))
    mixed_history = sum(depth_weights[0, j] * past[j] for j in range(HISTORY))
    hm0 = Chain(row_steps(mixed_history, row, core, flip))
    cot_chain = Chain(row_steps(cotangent, row, core, flip))

    saved = []
    mix = None
    for l in range(LAYERS):
        vec = vectors[l]
        outs = attention_forward(
            mix, x0 if l == 0 else None, vec, attn_w[l].parts(), cos, sin, segments
        )
        if l == 0:
            x = x0
        else:
            y0, x = outs[:2]
            outs = outs[2:]
        n1, st1, q, k, v, o, lse = outs[:7]
        left = list(outs[7:])
        if l == 0:
            left[0] = pin(left[0], expand_w[0].chain, reduce_w[0].chain, hm0)
        else:
            left[0] = pin(left[0], expand_w[1].chain, reduce_w[1].chain)
        right = swap_pieces(left)
        if l == 0:
            mid, n2, st2, u, act = mlp_forward(x, left, right, vec, expand_w[0].parts(), None)
            act = pin(act, attn_w[1].chain, reduce_w[0].chain)
            left = reduce_forward(act, reduce_w[0].parts())
            hm0 = hm0.finish()
            right = swap_pieces(left)
            right[0] = pin(right[0], attn_w[1].chain, expand_w[1].chain)
        else:
            mid, n2, st2, u, act, *left = mlp_forward(
                x, left, right, vec, expand_w[1].parts(), reduce_w[1].parts()
            )
            left[0] = pin(left[0], cot_chain)
            right = swap_pieces(left)
        saved.append((x, n1, st1, (q, k, v, o, lse), mid, n2, st2, u, act, left, right))
        mix = (depth_weights, hm0, mid, *left, *right, vec)

    cot = cot_chain.finish()
    mid1, left1, right1 = saved[1][4], saved[1][9], saved[1][10]

    def quarter_of(value, index):
        return lax.dynamic_slice_in_dim(value, index * part, part, 0)

    mine_at, sent_at = 2 * flip + core, 2 * (1 - flip) + core

    def tail_quarter(index):
        cut = lambda item: quarter_of(item, index).astype(F32)
        pick = lambda items: jnp.where(
            index < 2, jnp.where(index == 0, items[0], items[1]), jnp.where(index == 2, items[2], items[3])
        ).astype(F32)
        y1 = cut(mid1) + pick(left1) + pick(right1) + cut(vectors[1, REDUCE_B])[:, None]
        return (depth_weights[1, last] * cut(y0) + depth_weights[1, last + 1] * y1).astype(BF)

    chains = [{} for _ in range(LAYERS)]
    sums = [{} for _ in range(LAYERS)]
    for l in reversed(range(LAYERS)):
        x, n1, st1, heads, mid, n2, st2, u, act, y_left, y_right = saved[l]
        vec = vectors[l]
        aw, ew, rw = attn_w[l], expand_w[l], reduce_w[l]
        natural = l == 1
        count = 1 if natural else 2
        if l == 1:
            opening = (depth_weights, cot, mid, *y_left, *y_right, y0, vec)
            gyb, wide_sums, dots1, *grads = mlp_backward(
                place, natural, "last", opening, None, n2, u, act, 1, rw.other(), ew.other(), None
            )
        else:
            right[0] = pin(right[0], chains[1]["attn"])
            matrices = ("reduce", "expand", "attn")
            for name in matrices:
                chains[1][name].advance()
            right[0], sums_1 = lax.optimization_barrier(
                (right[0], [chains[1][name].held[0] for name in matrices])
            )
            sums_1 = lax.psum(sums_1, "dp")
            opening = (
                (depth_weights, cot, gmb, saved[1][0], saved[1][2], *left, *right, y0, vectors[1])
            )
            gyb, gx1, wide_sums, dots0, *grads = mlp_backward(
                place, natural, "first", opening, None, n2, u, act, 1, rw.other(), ew.other(), None
            )
            sums[1]["gain1"], sums[1]["shift1"] = wide_sums[8], wide_sums[16]
            gx1_home = Chain(home_steps(quarter_of(gx1, mine_at), quarter_of(gx1, sent_at), row))
        sums[l]["reduce_b"] = wide_sums[0]
        e_other, r_other = grads[:count], grads[count : 2 * count]
        be1, partial = grads[2 * count :]
        *grads, be0, l0, l1, l2, l3 = mlp_backward(
            place, natural, "own", None, gyb, n2, u, act, 0, rw.own, ew.own, partial
        )
        e_own, r_own, left = grads[:count], grads[count:], [l0, l1, l2, l3]
        if natural:
            right = swap_pieces(left)
            chains[l]["reduce"] = Chain(whole_steps(r_own[0], r_other[0]))
            chains[l]["expand"] = Chain(whole_steps(e_own[0], e_other[0]))
            right[0] = pin(right[0], chains[l]["reduce"])
        else:
            chains[l]["reduce"] = Chain(reduce_steps(r_own, r_other, bits))
            chains[l]["expand"] = Chain(reduce_steps(e_own, e_other, bits))
            left[0] = pin(left[0], chains[l]["reduce"])
            right = swap_pieces(left)
            right[0] = pin(right[0], chains[l]["reduce"])
        opening = (gyb, *left, *right, mid, st2, vec)
        gmb, wide_sums, *grads, db1, partial = attention_backward(
            place, natural, opening, None, n1, aw.other(), cos, sin, segments, heads, 1, None
        )
        a_other = grads
        sums[l]["gain2"], sums[l]["shift2"], sums[l]["merge_b"] = (
            wide_sums[0],
            wide_sums[8],
            wide_sums[16],
        )
        if l == 1:
            gmb = pin(gmb, chains[l]["expand"])
        else:
            chains[0]["expand"].advance()
            gmb = pin(gmb, chains[l]["reduce"], chains[l]["expand"])
        *grads, db0, l0, l1, l2, l3 = attention_backward(
            place, natural, None, gmb, n1, aw.own, cos, sin, segments, heads, 0, partial
        )
        left = [l0, l1, l2, l3]
        if l == 0:
            left[0] = pin(left[0], chains[0]["reduce"], chains[0]["expand"])
        right = swap_pieces(left)
        if natural:
            chains[l]["attn"] = Chain(whole_steps(grads[0], a_other[0]))
        else:
            chains[l]["attn"] = Chain(reduce_steps(grads, a_other, bits))
        sums[l]["pair"] = ((db0[0], be0[0]), (db1[0], be1[0]))
    chains[0]["attn"].advance()
    right[0] = pin(
        right[0], chains[0]["attn"], chains[0]["reduce"], chains[0]["expand"], gx1_home
    )
    gx0, wide_sums = final_backward(
        gmb, saved[0][0], saved[0][2], *left, *right, vectors[0]
    )
    sums[0]["gain1"], sums[0]["shift1"] = wide_sums[0], wide_sums[8]

    final = chains[0]["attn"]

    def onward(*others):
        *waiting, chains_now = others
        final.advance()
        for chain in chains_now:
            chain.advance()
        final.held, held, waiting = lax.optimization_barrier(
            (final.held, [chain.held for chain in chains_now], waiting)
        )
        for chain, value in zip(chains_now, held):
            chain.held = value
        return waiting

    ahead = (chains[0]["reduce"], chains[0]["expand"])
    gx0_home = Chain(home_steps(quarter_of(gx0, mine_at), quarter_of(gx0, sent_at), row))
    past, late_cot = onward(history, cotangent, ahead + (gx0_home,))
    g0_home = gx1_home.finish()
    input_grad = gx0_home.finish()
    history_out = []
    for j in range(HISTORY):
        term = depth_weights[0, j] * g0_home
        if j >= 1:
            term = term + depth_weights[1, j - 1] * late_cot
        history_out.append(term)

    past, late_cot, tail_mine, tail_sent = onward(
        past, late_cot, tail_quarter(mine_at), tail_quarter(sent_at), ahead
    )

    def by_core(value):
        return jnp.where(core == 0, jnp.sum(value), 0.0)

    mix0 = [jnp.sum(g0_home * past[j]) for j in range(HISTORY)] + [by_core(dots0[0])]
    mix1 = [jnp.sum(late_cot * past[j + 1]) for j in range(last)] + [
        by_core(dots1[0]),
        by_core(dots1[1]),
    ]
    mix_sum = jnp.concatenate([jnp.stack(mix0), jnp.stack(mix1)])
    mix_sum = mix_sum + swap_core(mix_sum)
    output_home = Chain(home_steps(tail_mine, tail_sent, row))
    (past,) = onward(past, ahead + (output_home,))
    output = sum(depth_weights[1, j] * past[j + 1] for j in range(last)) + output_home.finish()
    onward(ahead)
    (sums_1,) = onward(sums_1, ahead)

    names = ("gain1", "shift1", "gain2", "shift2", "merge_b", "reduce_b")
    lines = []
    for index, which in ((mine_at, 0), (sent_at, 1)):
        line = []
        for l in range(LAYERS):
            stacked = jnp.stack([sums[l][name] for name in names])
            cut = lax.dynamic_slice_in_dim(stacked, index * part, part, 1)
            line += [sums[l]["pair"][which][0], sums[l]["pair"][which][1], cut.reshape(-1)]
        lines.append(jnp.concatenate(line + [mix_sum]))
    total = lines[0] + swap_row(lines[1])
    for step in range(len(bits)):
        total = total + swap_dp(total, 1 << step)
    mix_grad = total[-mix_sum.shape[0] :].reshape(LAYERS, HISTORY + 1)
    per_layer = total[: -mix_sum.shape[0]].reshape(LAYERS, -1)
    wide_out = [per_layer[:, at + i * part : at + (i + 1) * part] for i in range(6)]

    attn_t = expand_t = reduce_t = None
    for l in reversed(range(LAYERS)):
        total = [chains[l][name].finish() for name in matrices] if l == 0 else sums_1
        reduce_t = assemble(total[0], place, l, [(LAYERS, units, width)], [units], False, reduce_t)
        expand_t = assemble(total[1], place, l, [(LAYERS, width, units)], [units], True, expand_t)
        attn_t = assemble(
            total[2],
            place,
            l,
            [(LAYERS, 3, part, width), (LAYERS, part, width)],
            [3 * part, part],
            False,
            attn_t,
        )
    return (
        output,
        input_grad,
        jnp.stack(history_out),
        attn_t[0],
        per_layer[:, : 3 * part].reshape(LAYERS, 3, part),
        attn_t[1],
        wide_out[4],
        wide_out[0],
        wide_out[1],
        wide_out[2],
        wide_out[3],
        expand_t[0],
        per_layer[:, 3 * part : at],
        reduce_t[0],
        wide_out[5],
        mix_grad,
    )


def solution(mesh):
    in_specs = (
        P("mp", "dp"),
        P(None, "mp", "dp"),
        P("dp", None),
        P("mp", "dp"),
        P(None, None, "mp", None),
        P(None, None, "mp"),
        P(None, "mp", None),
        P(None, "mp"),
        P(None, "mp"),
        P(None, "mp"),
        P(None, "mp"),
        P(None, "mp"),
        P(None, None, "mp"),
        P(None, "mp"),
        P(None, "mp", None),
        P(None, "mp"),
        P(),
    )
    out_specs = (
        P("mp", "dp"),
        P("mp", "dp"),
        P(None, "mp", "dp"),
        P(None, None, "mp", None),
        P(None, None, "mp"),
        P(None, "mp", None),
        P(None, "mp"),
        P(None, "mp"),
        P(None, "mp"),
        P(None, "mp"),
        P(None, "mp"),
        P(None, None, "mp"),
        P(None, "mp"),
        P(None, "mp", None),
        P(None, "mp"),
        P(),
    )
    return jax.shard_map(shards, mesh=mesh, in_specs=in_specs, out_specs=out_specs, check_vma=False)
```

```python
import functools

import jax
import jax.numpy as jnp
from jax import lax
from jax.experimental import pallas as pl
from jax.experimental.pallas import tpu as pltpu
from jax.sharding import PartitionSpec as P

HEAD = 64
HALF = HEAD // 2
LAYERS = 2
HISTORY = 4
EPS = 1e-05
MASKED = -1e30
BLK = 256
REACH = 512
TILE = 256
STRIP = 96
BF = jnp.bfloat16
F32 = jnp.float32
GELU_A = 0.7978845608028654
GELU_B = 0.044715
INPUT_ROWS, EXPAND_ROWS = (0, 3), (3, 7)
GAIN1, SHIFT1, GAIN2, SHIFT2, MERGE_B, REDUCE_B = 7, 8, 9, 10, 11, 12
TABLE_ROWS, TABLE_LANES = 16, 256
BIT, ROW, FLIP, CORE = 0, 1, 2, 3


def dot(a, b, on):
    return lax.dot_general(a, b, (on, ((), ())), preferred_element_type=F32)


def nn(a, b):
    return dot(a, b, ((1,), (0,)))


def nt(a, b):
    return dot(a, b, ((1,), (1,)))


def tn(a, b):
    return dot(a, b, ((0,), (0,)))


def full(shape):
    return pl.BlockSpec(shape, lambda t: (0,) * len(shape))


def shape(dims, kind=BF):
    return jax.ShapeDtypeStruct(dims, kind)


LATE, EARLY = "late", "early"


def launch(kernel, name, steps, ins, outs, scratch, micros, vmem, aliases=None):
    if steps == 1:
        ins = [(item, full(item.shape) if spec is LATE else spec) for item, spec in ins]
        outs = [(item, full(item.shape) if spec is EARLY else spec) for item, spec in outs]
    late = [i for i, (_, spec) in enumerate(ins) if spec is LATE]
    early = [i for i, (_, spec) in enumerate(outs) if spec is EARLY]
    anywhere = pl.BlockSpec(memory_space=pl.ANY)
    held = [pltpu.VMEM(ins[i][0].shape, ins[i][0].dtype) for i in late]
    held += [pltpu.VMEM(outs[i][0].shape, outs[i][0].dtype) for i in early]
    moves = len(held)

    def body(*refs):
        if not moves:
            kernel(*refs)
            return
        refs = list(refs)
        extra = refs[len(ins) + len(outs) + len(scratch) :]
        del refs[len(ins) + len(outs) + len(scratch) :]
        buffers, sems = extra[:moves], extra[moves]
        incoming, outgoing = [], []
        for slot, index in enumerate(late):
            incoming.append(pltpu.make_async_copy(refs[index], buffers[slot], sems.at[slot]))
            refs[index] = buffers[slot]
        for slot, index in enumerate(early, len(late)):
            index = len(ins) + index
            outgoing.append(pltpu.make_async_copy(buffers[slot], refs[index], sems.at[slot]))
            refs[index] = buffers[slot]
        step = pl.program_id(0)

        @pl.when(step == 0)
        def _():
            for move in incoming:
                move.start()

        @pl.when(step == steps - 1)
        def _():
            for move in incoming:
                move.wait()

        kernel(*refs)

        @pl.when(step == 0)
        def _():
            for move in outgoing:
                move.start()

        @pl.when(step == steps - 1)
        def _():
            for move in outgoing:
                move.wait()

    if moves:
        held.append(pltpu.SemaphoreType.DMA((moves,)))
    return pl.pallas_call(
        body,
        grid=(steps,),
        in_specs=[anywhere if spec is LATE else spec for _, spec in ins],
        out_specs=[anywhere if spec is EARLY else spec for _, spec in outs],
        out_shape=[struct for struct, _ in outs],
        scratch_shapes=list(scratch) + held,
        compiler_params=pltpu.CompilerParams(
            dimension_semantics=("arbitrary",), vmem_limit_bytes=vmem * 1024 * 1024
        ),
        cost_estimate=pl.CostEstimate(
            flops=int(micros * 1.0e9), bytes_accessed=1 << 20, transcendentals=0
        ),
        input_output_aliases=aliases or {},
        name=name,
    )(*[operand for operand, _ in ins])


def late(*operands):
    return [(operand, LATE) for operand in operands]


def out_early(dims, kind=BF):
    return (shape(dims, kind), EARLY)


def whole(*operands):
    return [(operand, full(operand.shape)) for operand in operands]


def scalars(operand):
    return [(operand, pl.BlockSpec(memory_space=pltpu.SMEM))]


def out_full(dims, kind=BF):
    return (shape(dims, kind), full(dims))


class Pieces:
    def __init__(self, refs):
        self.refs = refs
        self.size = refs[0].shape[0]

    def __getitem__(self, index):
        rows = index[0]
        at = rows.start // self.size
        return self.refs[at][slice(rows.start - at * self.size, rows.stop - at * self.size), :]

    def store(self, at, value):
        for start in range(0, value.shape[0], self.size):
            self.refs[(at + start) // self.size][...] = value[start : start + self.size].astype(BF)


def out_pieces(width, length):
    return [out_full((width // 4, length)) for _ in range(4)]


def choose(place, index, four, read):
    mine, theirs, core_mine, core_theirs = four
    here, side = divmod(index, 2)
    own = jnp.where(place[0, FLIP] == here, read(mine), read(theirs))
    other = jnp.where(place[0, FLIP] == here, read(core_mine), read(core_theirs))
    return jnp.where(place[0, CORE] == side, own, other)


class RowParts:
    def __init__(self, place, refs):
        self.place = place
        self.refs = refs
        self.size = refs[0].shape[0]

    def __getitem__(self, index):
        rows = index[0]
        at = rows.start // self.size
        cut = slice(rows.start - at * self.size, rows.stop - at * self.size)
        return choose(self.place, at, self.refs, lambda ref: ref[cut, :].astype(F32))


def columns_of(place, four, layer, part):
    return jnp.concatenate(
        [choose(place, q, four, lambda ref: ref[layer]).T[:part] for q in range(4)], 0
    )


def stacked_rows(ref, layer, rows, part):
    table = ref[layer].T[:part]
    return jnp.concatenate([table[:, row : row + 1] for row in range(*rows)], 0)


def strips(size):
    return [slice(at, at + STRIP) for at in range(0, size, STRIP)]


def key_range(block):
    return max(0, block * BLK - REACH), (block + 1) * BLK


def mask_shape(length):
    return (length // BLK, min(length, REACH + BLK), BLK)


def fill_mask(mask, segments, length):
    line = segments[...]
    column = jnp.broadcast_to(line, (8, length)).T[:, 0:1]
    for block in range(length // BLK):
        low, high = key_range(block)
        span = high - low
        here = line[:, block * BLK : high]
        there = column[low:high, :]
        query_pos = lax.broadcasted_iota(jnp.int32, (span, BLK), 1) + block * BLK
        key_pos = lax.broadcasted_iota(jnp.int32, (span, BLK), 0) + low
        allowed = (here == there) & (key_pos <= query_pos)
        mask[block, :span, :] = jnp.where(allowed, 0.0, MASKED)


def normalise(source, target, stats, columns, gain, shift, width, length):
    total = jnp.zeros((1, length), F32)
    squares = jnp.zeros((1, length), F32)
    for rows in strips(width):
        x = source(rows)
        total += jnp.sum(x, 0, keepdims=True)
        squares += jnp.sum(x * x, 0, keepdims=True)
    mean = total * (1.0 / width)
    scale = lax.rsqrt(squares * (1.0 / width) - mean * mean + EPS)
    stats[0:1, :] = mean
    stats[1:2, :] = scale
    return mean, scale


def apply_norm(x, mean, scale, columns, gain, shift, rows):
    return ((x - mean) * scale * columns[rows, gain : gain + 1] + columns[rows, shift : shift + 1]).astype(BF)


def norm_back(x, stats, left, right, base, gain, width, length, grad_n, grad_gain, emit):
    mean, scale = stats[0:1, :], stats[1:2, :]
    first = jnp.zeros((1, length), F32)
    second = jnp.zeros((1, length), F32)
    for rows in strips(width):
        hat = (x[rows, :].astype(F32) - mean) * scale
        grad = left[rows, :].astype(F32) + right[rows, :].astype(F32)
        grad_n[rows, :] = grad.astype(BF)
        product = grad * hat
        grad_gain[rows, :] = product.astype(BF)
        column = gain[rows]
        first += jnp.sum(grad * column, 0, keepdims=True)
        second += jnp.sum(product * column, 0, keepdims=True)
    first = first * (1.0 / width)
    second = second * (1.0 / width)
    for rows in strips(width):
        hat = (x[rows, :].astype(F32) - mean) * scale
        grad = left[rows, :].astype(F32) + right[rows, :].astype(F32)
        emit(rows, base(rows) + scale * (grad * gain[rows] - first - hat * second))


def row_sums(value):
    return nt(jnp.ones((8, value.shape[1]), BF), value)


def attention_forward_kernel(mixing, layer, heads, length, width, *refs):
    refs = list(refs)
    place = refs.pop(0)
    if mixing:
        coef, mid_i = refs[:2]
        left, right = Pieces(refs[2:6]), Pieces(refs[6:10])
        del refs[:10]
    incoming = RowParts(place, refs[:4])
    vectors = refs[4:8]
    a0d, a0r, a1d, a1r, cos, sin, segments = refs[8:15]
    del refs[:15]
    if mixing:
        y_o = refs.pop(0)
    x_o = refs.pop(0)
    n1_o, st_o, q_o, k_o, v_o, o_o, lse_o = refs[:7]
    part_o = Pieces(refs[7:11])
    lin, mask, o_all = refs[11:]
    head = pl.program_id(0)
    quarter = (heads // 2) * HEAD
    half = width // 2

    @pl.when(head == 0)
    def _():
        columns = columns_of(place, vectors, layer, width // 4)
        if mixing:
            bias = columns_of(place, vectors, layer - 1, width // 4)
            weight = coef[0, HISTORY]
            for rows in strips(width):
                y = (
                    mid_i[rows, :].astype(F32)
                    + left[rows, :].astype(F32)
                    + right[rows, :].astype(F32)
                    + bias[rows, REDUCE_B : REDUCE_B + 1]
                )
                y_o[rows, :] = y.astype(BF)
                x_o[rows, :] = (incoming[rows, :] + weight * y).astype(BF)
        else:
            for rows in strips(width):
                x_o[rows, :] = incoming[rows, :].astype(BF)
        source = x_o
        mean, scale = normalise(
            lambda rows: source[rows, :].astype(F32), None, st_o, None, None, None, width, length
        )
        for rows in strips(width):
            n1_o[rows, :] = apply_norm(
                source[rows, :].astype(F32), mean, scale, columns, GAIN1, SHIFT1, rows
            )
        for index, (d, r) in enumerate(((a0d, a0r), (a1d, a1r))):
            at = index * 3 * quarter
            lin[at : at + 3 * quarter, :] = (
                nn(d[: 3 * quarter, :], n1_o[:half, :])
                + nn(r[: 3 * quarter, :], n1_o[half:, :])
                + stacked_rows(vectors[index], layer, INPUT_ROWS, width // 4)
            )
        fill_mask(mask, segments, length)

    c, s = cos[...], sin[...]
    group = head // (heads // 2)
    base = group * 3 * quarter + (head - group * (heads // 2)) * HEAD

    def rope(start):
        first = lin[pl.ds(pl.multiple_of(start, HALF), HALF), :]
        second = lin[pl.ds(pl.multiple_of(start + HALF, HALF), HALF), :]
        return jnp.concatenate([first * c - second * s, second * c + first * s], 0)

    q = (rope(base).astype(BF) * BF(HEAD**-0.5)).astype(BF)
    key = rope(base + quarter).astype(BF)
    v = lin[pl.ds(pl.multiple_of(base + 2 * quarter, HEAD), HEAD), :].astype(BF)
    q_o[0] = q
    k_o[0] = key
    v_o[0] = v
    for block in range(length // BLK):
        low, high = key_range(block)
        cols = slice(block * BLK, high)
        scores = tn(key[:, low:high], q[:, cols]) + mask[block, : high - low, :]
        peak = jnp.max(scores, 0, keepdims=True)
        weights = jnp.exp(scores - peak)
        total = jnp.sum(weights, 0, keepdims=True)
        out = (nn(v[:, low:high], weights.astype(BF)) * (1.0 / total)).astype(BF)
        o_o[0, :, cols] = out
        o_all[pl.ds(pl.multiple_of(head * HEAD, HEAD), HEAD), cols] = out
        lse_o[0, :, cols] = peak + jnp.log(total)

    @pl.when(head == heads - 1)
    def _():
        for at, own, other in ((0, a0d, a1d), (half, a0r, a1r)):
            part_o.store(
                at,
                tn(own[3 * quarter :, :], o_all[:quarter, :])
                + tn(other[3 * quarter :, :], o_all[quarter:, :]),
            )


def attention_forward(place, mix, incoming, vectors, layer, weights, cos, sin, segments):
    length = segments.shape[1]
    rows, half = weights[0].shape
    width = 2 * half
    quarter = rows // 4
    heads = 2 * quarter // HEAD
    ins = scalars(place)
    outs = [out_early((width, length))]
    if mix is not None:
        ins = ins + scalars(mix[0]) + whole(*mix[1:])
        outs = outs * 2
    ins = ins + whole(*incoming, *vectors, *weights, cos, sin, segments)
    per_head = lambda size: pl.BlockSpec((1, size, length), lambda h: (h, 0, 0))
    heads_out = (shape((heads, HEAD, length)), per_head(HEAD))
    outs = outs + [
        out_early((width, length)),
        out_full((8, length), F32),
        heads_out,
        heads_out,
        heads_out,
        heads_out,
        (shape((heads, 1, length), F32), per_head(1)),
    ]
    outs = outs + out_pieces(width, length)
    return launch(
        functools.partial(
            attention_forward_kernel, mix is not None, layer, heads, length, width
        ),
        "attention_forward",
        heads,
        ins,
        outs,
        [
            pltpu.VMEM((6 * quarter, length), F32),
            pltpu.VMEM(mask_shape(length), F32),
            pltpu.VMEM((2 * quarter, length), BF),
        ],
        20,
        58,
    )


def halves_of(refs, natural, place, half):
    if not natural:
        return [lambda index, value, ref=ref: ref.__setitem__(index, value.astype(BF)) for ref in refs]

    def at(which):
        cols = pl.ds(pl.multiple_of((place[0, 0] ^ which) * half, half), half)

        def put(index, value):
            refs[0][index[:-1] + (cols,)] = value.astype(BF)

        return put

    return [at(0), at(1)]


def attention_backward_kernel(opening, layer, natural, heads, length, width, *refs):
    refs = list(refs)
    place = refs.pop(0)
    if opening:
        grad_i, mid, st, vectors = refs[0], refs[9], refs[10], refs[11:15]
        left, right = Pieces(refs[1:5]), Pieces(refs[5:9])
        del refs[:15]
    else:
        gmb = refs.pop(0)
    n1, ad, ar, cos, sin, segments, q_i, k_i, v_i, o_i, lse_i = refs[:11]
    del refs[:11]
    if opening:
        gmb, sums_o = refs[:2]
        del refs[:2]
    else:
        add = refs.pop(0)
    count = 1 if natural else 2
    put = halves_of(refs[:count], natural, place, width // 2)
    db_o = refs[count]
    del refs[: count + 1]
    if opening:
        part_o = refs.pop(0)
    else:
        part_o = Pieces(refs[:4])
        del refs[:4]
    mask, go_all, gl_all, gk_s, gv_s = refs[:5]
    del refs[:5]
    head = pl.program_id(0)
    quarter = heads * HEAD
    half = width // 2

    @pl.when(head == 0)
    def _():
        if opening:
            grad_n, grad_gain = refs
            columns = columns_of(place, vectors, layer, width // 4)
            norm_back(
                mid,
                st,
                left,
                right,
                lambda rows: grad_i[rows, :].astype(F32),
                columns[:, GAIN2 : GAIN2 + 1],
                width,
                length,
                grad_n,
                grad_gain,
                lambda rows, value: gmb.__setitem__((rows, slice(None)), value.astype(BF)),
            )
            sums_o[0:8, :] = row_sums(grad_gain[...])
            sums_o[8:16, :] = row_sums(grad_n[...])
            sums_o[16:24, :] = row_sums(gmb[...])
        go_all[...] = (
            nn(ad[3 * quarter :, :], gmb[:half, :]) + nn(ar[3 * quarter :, :], gmb[half:, :])
        ).astype(BF)
        o_flat = o_i[...].reshape(quarter, length)
        below = (slice(3 * quarter, 4 * quarter), slice(None))
        put[0](below, nt(o_flat, gmb[:half, :]))
        put[1](below, nt(o_flat, gmb[half:, :]))
        fill_mask(mask, segments, length)

    base = pl.multiple_of(head * HEAD, HEAD)
    q, key, v = q_i[0], k_i[0], v_i[0]
    go = go_all[pl.ds(base, HEAD), :]
    delta = jnp.sum(go.astype(F32) * o_i[head].astype(F32), 0, keepdims=True)
    gk_s[...] = jnp.zeros_like(gk_s)
    gv_s[...] = jnp.zeros_like(gv_s)
    gq_parts = []
    for block in range(length // BLK):
        low, high = key_range(block)
        cols = slice(block * BLK, high)
        scores = tn(key[:, low:high], q[:, cols]) + mask[block, : high - low, :]
        probs = jnp.exp(scores - lse_i[0, :, cols])
        grad_probs = tn(v[:, low:high], go[:, cols])
        grad_scores = (probs * (grad_probs - delta[:, cols])).astype(BF)
        gv_s[:, low:high] += nt(go[:, cols], probs.astype(BF))
        gk_s[:, low:high] += nt(q[:, cols], grad_scores)
        gq_parts.append(nn(key[:, low:high], grad_scores))
    c, s = cos[...], sin[...]

    def store(part, top, bottom):
        start = pl.multiple_of(part * quarter + base, HEAD)
        gl_all[pl.ds(start, HEAD), :] = jnp.concatenate([top, bottom], 0).astype(BF)

    gq = jnp.concatenate(gq_parts, 1) * HEAD**-0.5
    store(0, gq[:HALF] * c + gq[HALF:] * s, gq[HALF:] * c - gq[:HALF] * s)
    gk = gk_s[...]
    store(1, gk[:HALF] * c + gk[HALF:] * s, gk[HALF:] * c - gk[:HALF] * s)
    store(2, gv_s[:HALF, :], gv_s[HALF:, :])

    @pl.when(head == heads - 1)
    def _():
        db_o[...] = row_sums(gl_all[...])
        above = (slice(0, 3 * quarter), slice(None))
        put[0](above, nt(gl_all[...], n1[:half, :]))
        put[1](above, nt(gl_all[...], n1[half:, :]))
        for at, w in ((0, ad), (half, ar)):
            value = tn(w[: 3 * quarter, :], gl_all[...])
            if opening:
                part_o[at : at + half, :] = value.astype(BF)
            else:
                part_o.store(at, value + add[at : at + half, :].astype(F32))


def attention_backward(place, layer, natural, opening, gmb, n1, weights, cos, sin, segments, saved, group, add):
    length = segments.shape[1]
    rows, half = weights[0].shape
    width = 2 * half
    quarter = rows // 4
    heads = quarter // HEAD
    q, key, v, o, lse = saved
    if opening is not None:
        ins = scalars(place) + whole(*opening)
        outs = [out_early((width, length)), out_full((24, width), F32)]
        scratch = [pltpu.VMEM((width, length), BF), pltpu.VMEM((width, length), BF)]
    else:
        ins = scalars(place) + whole(gmb)
        outs = []
        scratch = []
    at = group * heads
    per_head = lambda size: pl.BlockSpec((1, size, length), lambda h: (at + h, 0, 0))
    ins = ins + late(n1) + whole(*weights, cos, sin, segments)
    ins = ins + [(item, per_head(HEAD)) for item in (q, key, v)]
    ins = ins + [(o, pl.BlockSpec((heads, HEAD, length), lambda h: (group, 0, 0))), (lse, per_head(1))]
    if add is not None:
        ins = ins + late(add)
    outs = outs + ([out_full((rows, width))] if natural else [out_full((rows, half))] * 2)
    outs = outs + [out_full((8, 3 * quarter), F32)]
    outs = outs + (out_pieces(width, length) if add is not None else [out_full((width, length))])
    return launch(
        functools.partial(
            attention_backward_kernel, opening is not None, layer, natural, heads, length, width
        ),
        "attention_backward",
        heads,
        ins,
        outs,
        [
            pltpu.VMEM(mask_shape(length), F32),
            pltpu.VMEM((quarter, length), BF),
            pltpu.VMEM((3 * quarter, length), BF),
            pltpu.VMEM((HEAD, length), F32),
            pltpu.VMEM((HEAD, length), F32),
        ]
        + scratch,
        14,
        58,
    )


def mlp_forward_kernel(merged, layer, tiles, length, width, *refs):
    refs = list(refs)
    place = refs.pop(0)
    x, left, right, vectors = refs[0], Pieces(refs[1:5]), Pieces(refs[5:9]), refs[9:13]
    e0d, e0r, e1d, e1r = refs[13:17]
    del refs[:17]
    if merged:
        r0d, r0r, r1d, r1r = refs[:4]
        del refs[:4]
    mid_o, n2_o, st_o, u_o, act_o = refs[:5]
    del refs[:5]
    columns_s = refs.pop(0 if not merged else 4)
    if merged:
        part_o, acts = Pieces(refs[:4]), refs[4]
    t = pl.program_id(0)
    half = width // 2
    units = tiles * TILE

    @pl.when(t == 0)
    def _():
        columns = columns_of(place, vectors, layer, width // 4)
        for index in range(2):
            columns_s[:, index : index + 1] = stacked_rows(
                vectors[index], layer, EXPAND_ROWS, width // 4
            )
        for rows in strips(width):
            mid_o[rows, :] = (
                x[rows, :].astype(F32)
                + left[rows, :].astype(F32)
                + right[rows, :].astype(F32)
                + columns[rows, MERGE_B : MERGE_B + 1]
            ).astype(BF)
        mean, scale = normalise(
            lambda rows: mid_o[rows, :].astype(F32), None, st_o, None, None, None, width, length
        )
        for rows in strips(width):
            n2_o[rows, :] = apply_norm(
                mid_o[rows, :].astype(F32), mean, scale, columns, GAIN2, SHIFT2, rows
            )

    def expand(group, d, r):
        at = pl.multiple_of((t - group * tiles) * TILE, TILE)
        bias = columns_s[pl.ds(at, TILE), group : group + 1]
        u = tn(d[...], n2_o[:half, :]) + tn(r[...], n2_o[half:, :]) + bias
        act = (0.5 * u * (1.0 + jnp.tanh(GELU_A * (u + GELU_B * (u * u * u))))).astype(BF)
        u_o[...] = u.astype(BF)
        act_o[...] = act
        if merged:
            acts[pl.ds(pl.multiple_of(t * TILE, TILE), TILE), :] = act

    @pl.when(t < tiles)
    def _():
        expand(0, e0d, e0r)

    @pl.when(t >= tiles)
    def _():
        expand(1, e1d, e1r)

    if merged:

        @pl.when(t == 2 * tiles - 1)
        def _():
            for at, own, other in ((0, r0d, r1d), (half, r0r, r1r)):
                part_o.store(at, tn(own[...], acts[:units, :]) + tn(other[...], acts[units:, :]))


def mlp_forward(place, x, left, right, vectors, layer, expand, reduce):
    width, length = x.shape
    half, units = expand[0].shape
    tiles = units // TILE
    merged = reduce is not None
    first = pl.BlockSpec((half, TILE), lambda t: (0, jnp.minimum(t, tiles - 1)))
    second = pl.BlockSpec((half, TILE), lambda t: (0, jnp.maximum(t - tiles, 0)))
    ins = scalars(place) + whole(x, *left, *right, *vectors)
    ins = ins + list(zip(expand, (first, first, second, second)))
    per_tile = (shape((2 * units, length)), pl.BlockSpec((TILE, length), lambda t: (t, 0)))
    outs = [
        out_early((width, length)),
        out_early((width, length)),
        out_full((8, length), F32),
        per_tile,
        per_tile,
    ]
    scratch = [pltpu.VMEM((units, 128), F32)]
    if merged:
        ins = ins + late(*reduce)
        outs = outs + out_pieces(width, length)
        scratch = scratch + [pltpu.VMEM((2 * units, length), BF)]
    return launch(
        functools.partial(mlp_forward_kernel, merged, layer, tiles, length, width),
        "mlp_forward",
        2 * tiles,
        ins,
        outs,
        scratch,
        14 if merged else 10,
        58,
    )


def reduce_forward_kernel(units, half, act, *refs):
    r0d, r0r, r1d, r1r = refs[:4]
    part_o = Pieces(refs[4:])
    for at, own, other in ((0, r0d, r1d), (half, r0r, r1r)):
        part_o.store(at, tn(own[...], act[:units, :]) + tn(other[...], act[units:, :]))


def reduce_forward(act, reduce):
    units, half = reduce[0].shape
    length = act.shape[1]
    return launch(
        functools.partial(reduce_forward_kernel, units, half),
        "reduce_forward",
        1,
        whole(act, *reduce),
        out_pieces(2 * half, length),
        [],
        4,
        32,
    )


def mlp_backward_kernel(mode, layer, natural, tiles, length, width, *refs):
    refs = list(refs)
    place = refs.pop(0)
    half = width // 2
    units = tiles * TILE
    if mode == "last":
        coef, mid = refs[:2]
        left, right = Pieces(refs[2:6]), Pieces(refs[6:10])
        y0, vectors = refs[10], refs[11:15]
        cot = RowParts(place, refs[15:19])
        del refs[:19]
    elif mode == "first":
        coef, cot, gmid, x, st = refs[:5]
        left, right = Pieces(refs[5:9]), Pieces(refs[9:13])
        y0, vectors = refs[13], refs[14:18]
        del refs[:18]
    else:
        gyb = refs.pop(0)
    n2, u_i, act, rd, rr, ed, er = refs[:7]
    del refs[:7]
    if mode == "own":
        add = refs.pop(0)
    else:
        gyb = refs.pop(0)
        if mode == "first":
            gx_o = refs.pop(0)
        else:
            cot_o, tail_o = refs[:2]
            del refs[:2]
        sums_o, dots_o = refs[:2]
        del refs[:2]
    count = 1 if natural else 2
    put_expand = halves_of(refs[:count], natural, place, half)
    put_reduce = halves_of(refs[count : 2 * count], natural, place, half)
    be_o = refs[2 * count]
    del refs[: 2 * count + 1]
    if mode == "own":
        part_o = Pieces(refs[:4])
        del refs[:4]
    else:
        part_o = refs.pop(0)
    gubs = refs.pop(0)
    t = pl.program_id(0)

    if mode != "own":

        @pl.when(t == 0)
        def _():
            columns = columns_of(place, vectors, layer, width // 4)
            dots_o[...] = jnp.zeros_like(dots_o)
            if mode == "last":
                for rows in strips(width):
                    value = cot[rows, :]
                    cot_o[rows, :] = value.astype(BF)
                    gyb[rows, :] = (coef[1, HISTORY] * value).astype(BF)
                    y1 = (
                        mid[rows, :].astype(F32)
                        + left[rows, :].astype(F32)
                        + right[rows, :].astype(F32)
                        + columns[rows, REDUCE_B : REDUCE_B + 1]
                    )
                    first = y0[rows, :].astype(F32)
                    tail_o[rows, :] = (coef[1, HISTORY - 1] * first + coef[1, HISTORY] * y1).astype(BF)
                    dots_o[0:1, :] += jnp.sum(value * first, 0, keepdims=True)
                    dots_o[1:2, :] += jnp.sum(value * y1, 0, keepdims=True)
                sums_o[0:8, :] = row_sums(gyb[...])
            else:
                grad_n, grad_gain = refs

                def emit(rows, value):
                    gx_o[rows, :] = value.astype(BF)
                    gyb[rows, :] = (
                        coef[1, HISTORY - 1] * cot[rows, :].astype(F32) + coef[0, HISTORY] * value
                    ).astype(BF)
                    dots_o[0:1, :] += jnp.sum(value * y0[rows, :].astype(F32), 0, keepdims=True)

                norm_back(
                    x,
                    st,
                    left,
                    right,
                    lambda rows: gmid[rows, :].astype(F32),
                    columns[:, GAIN1 : GAIN1 + 1],
                    width,
                    length,
                    grad_n,
                    grad_gain,
                    emit,
                )
                sums_o[0:8, :] = row_sums(gyb[...])
                sums_o[8:16, :] = row_sums(grad_gain[...])
                sums_o[16:24, :] = row_sums(grad_n[...])

    ga = nn(rd[...], gyb[:half, :]) + nn(rr[...], gyb[half:, :])
    u = u_i[...].astype(F32)
    square = u * u
    th = jnp.tanh(GELU_A * u * (1.0 + GELU_B * square))
    slope = 0.5 * (1.0 + th) + (0.5 * GELU_A) * u * (1.0 - th * th) * (1.0 + (3.0 * GELU_B) * square)
    gub = (ga * slope).astype(BF)
    gubs[pl.ds(pl.multiple_of(t * TILE, TILE), TILE), :] = gub
    be_o[...] = row_sums(gub)
    every = (slice(None), slice(None))
    for index, rows in enumerate((slice(0, half), slice(half, width))):
        put_expand[index](every, nt(gub, n2[rows, :]))
        put_reduce[index](every, nt(act[...], gyb[rows, :]))

    @pl.when(t == tiles - 1)
    def _():
        for at, w in ((0, ed), (half, er)):
            value = nn(w[...], gubs[...])
            if mode == "own":
                part_o.store(at, value + add[at : at + half, :].astype(F32))
            else:
                part_o[at : at + half, :] = value.astype(BF)


def mlp_backward(place, layer, natural, mode, opening, gyb, n2, u, act, group, reduce, expand, add):
    width, length = n2.shape
    half, units = expand[0].shape
    tiles = units // TILE
    outs = []
    scratch = [pltpu.VMEM((units, length), BF)]
    if mode == "own":
        ins = scalars(place) + whole(gyb)
    else:
        ins = scalars(place) + scalars(opening[0]) + whole(*opening[1:])
        outs = outs + [out_early((width, length)), out_early((width, length))]
        if mode == "last":
            outs = outs + [out_early((width, length))]
        if mode == "first":
            scratch = scratch + [pltpu.VMEM((width, length), BF), pltpu.VMEM((width, length), BF)]
        outs = outs + [out_full((24, width), F32), out_full((8, length), F32)]
    at = group * tiles
    per_tile = pl.BlockSpec((TILE, length), lambda t: (at + t, 0))
    reduce_tile = pl.BlockSpec((TILE, half), lambda t: (t, 0))
    ins = ins + whole(n2) + [(u, per_tile), (act, per_tile)]
    ins = ins + [(item, reduce_tile) for item in reduce] + late(*expand)
    if add is not None:
        ins = ins + late(add)
    if natural:
        outs = outs + [(shape((units, width)), pl.BlockSpec((TILE, width), lambda t: (t, 0)))] * 2
    else:
        outs = outs + [(shape((units, half)), reduce_tile)] * 4
    outs = outs + [
        (shape((8, units), F32), pl.BlockSpec((8, TILE), lambda t: (0, t))),
    ]
    outs = outs + (out_pieces(width, length) if add is not None else [out_full((width, length))])
    return launch(
        functools.partial(mlp_backward_kernel, mode, layer, natural, tiles, length, width),
        "mlp_backward",
        tiles,
        ins,
        outs,
        scratch,
        13,
        58,
    )


def final_kernel(length, width, place, *refs):
    gmid, x, st = refs[:3]
    left, right = Pieces(refs[3:7]), Pieces(refs[7:11])
    vectors = refs[11:15]
    gx_o, sums_o, grad_n, grad_gain = refs[15:]
    columns = columns_of(place, vectors, 0, width // 4)
    norm_back(
        x,
        st,
        left,
        right,
        lambda rows: gmid[rows, :].astype(F32),
        columns[:, GAIN1 : GAIN1 + 1],
        width,
        length,
        grad_n,
        grad_gain,
        lambda rows, value: gx_o.__setitem__((rows, slice(None)), value.astype(BF)),
    )
    sums_o[0:8, :] = row_sums(grad_gain[...])
    sums_o[8:16, :] = row_sums(grad_n[...])


def final_backward(place, *operands):
    width, length = operands[0].shape
    return launch(
        functools.partial(final_kernel, length, width),
        "norm_backward",
        1,
        scalars(place) + whole(*operands),
        [out_full((width, length)), out_full((16, width), F32)],
        [pltpu.VMEM((width, length), BF), pltpu.VMEM((width, length), BF)],
        5,
        32,
    )


def finish_kernel(entries, place, coef, history, cot, *refs):
    tail, g0, gx0 = refs[0:2], refs[2:4], refs[4:6]
    output, input_grad, history_grad, dots, total = refs[6:]
    step = pl.program_id(0)
    length = tail[0].shape[1]
    halves = [
        pl.ds(pl.multiple_of((place[0, ROW] ^ which) * length, length), length)
        for which in range(2)
    ]
    behind = coef[1, jnp.maximum(step - 1, 0)]
    carried = jnp.where(step == 0, 0.0, behind)

    @pl.when(step == 0)
    def _():
        total[...] = jnp.zeros_like(total)
        for cols, part in zip(halves, gx0):
            input_grad[:, cols] = part[...].astype(F32)

    entry = history[0]
    total[...] += carried * entry
    dots[0, 4:8, :] = jnp.broadcast_to(jnp.sum(cot[...] * entry, 0, keepdims=True), (4, 2 * length))
    for cols, part in zip(halves, g0):
        grad = part[...].astype(F32)
        history_grad[0, :, cols] = coef[0, step] * grad + carried * cot[:, cols]
        dots[0, 0:4, cols] = jnp.broadcast_to(
            jnp.sum(grad * history[0, :, cols], 0, keepdims=True), (4, length)
        )

    @pl.when(step == entries - 1)
    def _():
        for cols, part in zip(halves, tail):
            output[:, cols] = total[:, cols] + part[...].astype(F32)


def finish(place, coef, history, cot, tail, g0, gx0):
    entries, part, tokens = history.shape
    block = pl.BlockSpec((1, part, tokens), lambda t: (t, 0, 0))
    return launch(
        functools.partial(finish_kernel, entries),
        "finish",
        entries,
        scalars(place) + scalars(coef) + [(history, block)] + whole(cot, *tail, *g0, *gx0),
        [
            out_full((part, tokens), F32),
            out_full((part, tokens), F32),
            (shape((entries, part, tokens), F32), block),
            (
                shape((entries, 8, tokens), F32),
                pl.BlockSpec((1, 8, tokens), lambda t: (t, 0, 0)),
            ),
        ],
        [pltpu.VMEM((part, tokens), F32)],
        6,
        40,
    )


def lines_kernel(wide, part, mine_at, sent_at, place, *refs):
    count = len(wide)
    sums, pairs = refs[:count], refs[count : count + 8]
    mix, mine_o, sent_o = refs[count + 8 :]
    for out, which, index in ((mine_o, 0, place[0, mine_at]), (sent_o, 1, place[0, sent_at])):
        out[...] = jnp.zeros_like(out)
        for at, (ref, row) in enumerate(zip(sums, wide)):
            line = ref[row : row + 1, :]
            cut = line[:, :part]
            for q in range(1, 4):
                cut = jnp.where(index == q, line[:, q * part : (q + 1) * part], cut)
            out[at : at + 1, :part] = cut
        for l in range(LAYERS):
            for k in range(2):
                line = pairs[4 * l + 2 * which + k][0:1, :]
                out[count + 2 * l + k : count + 2 * l + k + 1, : line.shape[1]] = line
        at = count + 2 * LAYERS
        out[at : at + 1, : mix.shape[1]] = mix[0:1, :]


def vector_lines(place, wide, pairs, mix, width, part):
    rows = -(-(len(wide) + 2 * LAYERS + 1) // 8) * 8
    return launch(
        functools.partial(lines_kernel, [row for _, row in wide], part, 4, 5),
        "vector_lines",
        1,
        scalars(place) + whole(*[item for item, _ in wide], *pairs, mix),
        [out_full((rows, width), F32)] * 2,
        [],
        2,
        16,
    )


def swap_core(value):
    size = lax.axis_size("mp")
    return lax.ppermute(value, "mp", [(i, i ^ 1) for i in range(size)])


def swap_row(value):
    size = lax.axis_size("mp")
    return lax.ppermute(value, "mp", [(i, i ^ 2) for i in range(size)])


def swap_dp(value, bit):
    size = lax.axis_size("dp")
    return lax.ppermute(value, "dp", [(i, i ^ bit) for i in range(size)])


def half_of(value, which, axis=0):
    size = value.shape[axis] // 2
    return lax.dynamic_slice_in_dim(value, which * size, size, axis)


def ordered(mine, theirs, which, axis=0):
    return jnp.where(
        which == 0,
        jnp.concatenate([mine, theirs], axis),
        jnp.concatenate([theirs, mine], axis),
    )


def cast_kernel(kinds, place, *refs):
    refs = list(refs)
    outs = refs[-2 * len(kinds) :]
    for index, kind in enumerate(kinds):
        near_o, far_o = outs[2 * index : 2 * index + 2]
        for out, which in ((near_o, 0), (far_o, 1)):
            if kind == "expand":
                half = out.shape[0]
                rows = pl.ds(pl.multiple_of((place[0, BIT] ^ which) * half, half), half)
                out[...] = refs[0][0, rows, :].astype(BF)
                continue
            half = out.shape[1]
            cols = pl.ds(pl.multiple_of((place[0, BIT] ^ which) * half, half), half)
            if kind == "reduce":
                out[...] = refs[0][0, :, cols].astype(BF)
                continue
            part = refs[1].shape[1]
            for k in range(3):
                out[k * part : (k + 1) * part, :] = refs[0][0, k, :, cols].astype(BF)
            out[3 * part :, :] = refs[1][0, :, cols].astype(BF)
        del refs[: 2 if kind == "attn" else 1]


def cast_weights(place, layer, kinds, operands):
    ins = scalars(place)
    for item in operands:
        block = (1,) + item.shape[1:]
        ins.append(
            (item, pl.BlockSpec(block, lambda t, n=len(block): (layer,) + (0,) * (n - 1)))
        )
    outs = []
    for kind in kinds:
        if kind == "attn":
            dims = (4 * operands[0].shape[2], operands[0].shape[3] // 2)
        elif kind == "expand":
            dims = (operands[-2].shape[1] // 2, operands[-2].shape[2])
        else:
            dims = (operands[-1].shape[1], operands[-1].shape[2] // 2)
        outs += [out_full(dims), out_full(dims)]
    found = launch(
        functools.partial(cast_kernel, kinds), "cast", 1, ins, outs, [], 2 * len(kinds), 40
    )
    return [tuple(found[i : i + 2]) for i in range(0, len(found), 2)]


def split_rows_kernel(entries, place, *refs):
    if entries:
        coef, value, mine, sent, total = refs
        step = pl.program_id(0)

        @pl.when(step == 0)
        def _():
            total[...] = coef[0, 0] * value[0]

        @pl.when(step > 0)
        def _():
            total[...] += coef[0, step] * value[0]

        source = total
    else:
        source, mine, sent = refs
    length = mine.shape[1]
    for out, which in ((mine, 0), (sent, 1)):
        cols = pl.ds(pl.multiple_of((place[0, ROW] ^ which) * length, length), length)
        if entries:

            @pl.when(step == entries - 1)
            def _():
                out[...] = source[:, cols].astype(BF)

        else:
            out[...] = source[:, cols].astype(BF)


def split_rows(place, value, coef=None):
    part, tokens = value.shape[-2:]
    ins = scalars(place)
    if coef is None:
        steps, entries = 1, 0
        ins = ins + whole(value)
        scratch = []
    else:
        steps = entries = value.shape[0]
        ins = ins + scalars(coef) + [(value, pl.BlockSpec((1, part, tokens), lambda t: (t, 0, 0)))]
        scratch = [pltpu.VMEM((part, tokens), F32)]
    return launch(
        functools.partial(split_rows_kernel, entries),
        "split_rows",
        steps,
        ins,
        [out_full((part, tokens // 2))] * 2,
        scratch,
        2,
        24,
    )


def gather_steps(mine, sent):
    theirs, core_mine = yield [swap_row(sent), swap_core(mine)]
    (core_theirs,) = yield [swap_core(theirs)]
    yield [mine, theirs, core_mine, core_theirs]


def home_steps(mine, sent, row):
    (theirs,) = yield [swap_row(sent)]
    yield mine, theirs


def fetch_steps(near, far, relay):
    (direct,) = yield [swap_row(near)]
    (rest,) = yield [swap_dp(direct, 1) if relay else swap_row(far)]
    yield direct, rest


class Weight:
    def __init__(self, near, far, relay=True):
        self.own = (near, far)
        self.chain = Chain(fetch_steps(near, far, relay))

    def other(self):
        return self.chain.finish()

    def parts(self):
        return self.own + tuple(self.other())


def swap_pieces(pieces):
    return [swap_core(piece) for piece in pieces]


def add_kernel(count, *refs):
    for a, b, out in zip(refs[:count], refs[count : 2 * count], refs[2 * count :]):
        out[...] = (a[...].astype(F32) + b[...].astype(F32)).astype(BF)


def add_all(mine, theirs):
    return launch(
        functools.partial(add_kernel, len(mine)),
        "add",
        1,
        whole(*mine, *theirs),
        [out_full(item.shape) for item in mine],
        [],
        2,
        16,
    )


def add_low(mine, theirs):
    return (mine.astype(F32) + theirs.astype(F32)).astype(BF)


def assemble_kernel(turned, counts, halves, pick, *refs):
    if halves:
        place, near, far = refs[:3]
        scratch = refs[-1]
        outs = refs[len(refs) - 1 - len(counts) : -1]
        half = near.shape[1]
        a, b = near[...].astype(F32), far[...].astype(F32)
        first = place[0, 0] == 0
        scratch[:, :half] = jnp.where(first, a, b)
        scratch[:, half:] = jnp.where(first, b, a)
    else:
        place, near, far = refs[:3]
        outs = refs[len(refs) - len(counts) :]
        scratch = jnp.where(place[0, BIT] == pick, near[...].astype(F32), far[...].astype(F32))
    at = 0
    for out, count in zip(outs, counts):
        value = scratch[at : at + count, :].astype(F32)
        out[...] = (value.T if turned else value).reshape(out.shape)
        at += count


def assemble(total, place, layer, shapes, counts, turned, held):
    halves = not isinstance(total[1], int)
    pick = 0
    if halves:
        ins = scalars(place) + whole(*total)
    else:
        total, pick = total
        ins = scalars(place) + whole(*total)
    aliases = {}
    if held is not None:
        for index, item in enumerate(held):
            aliases[len(ins)] = index
            ins.append((item, pl.BlockSpec(memory_space=pl.ANY)))
    outs = []
    for dims in shapes:
        block = pl.BlockSpec((1,) + dims[1:], lambda t, dims=dims: (layer,) + (0,) * (len(dims) - 1))
        outs.append((shape(dims, F32), block))
    rows = sum(counts)
    scratch = [pltpu.VMEM((rows, 2 * total[0].shape[1]), F32)] if halves else []
    return launch(
        functools.partial(assemble_kernel, turned, counts, halves, pick),
        "assemble",
        1,
        ins,
        outs,
        scratch,
        3,
        24,
        aliases,
    )


def reduce_steps(own, other, bits):
    (near,) = yield [swap_row(other[0])]
    near, far = yield [near, swap_row(other[1])]
    near, far = add_all(own, (near, far))
    got = yield [swap_dp(far, 1)]
    (value,) = add_all((near,), got)
    for step in range(1, len(bits)):
        away = half_of(value, 1 - bits[step])
        got = yield [swap_dp(away, 1 << step)]
        value = add_low(half_of(value, bits[step]), got[0])
    for step in reversed(range(1, len(bits))):
        got = yield [swap_dp(value, 1 << step)]
        value = ordered(value, got[0], bits[step])
    got = yield [swap_dp(value, 1)]
    yield value, got[0]


def half_steps(items):
    got = []
    for item in items:
        *got, last = yield got + [swap_row(item)]
        got = got + [last]


def reversed_bits(index, count):
    return sum(((index >> k) & 1) << (count - 1 - k) for k in range(count))


def add_stack_kernel(count, bits, place, *refs):
    out = refs[-1]
    size, half = refs[0].shape
    block = out.shape[0] >> bits
    for index in range(count):
        a, b = refs[index], refs[count + index]
        cols = pl.ds(pl.multiple_of((place[0, BIT] ^ (index % 2)) * half, half), half)
        for start in range(0, size, block):
            to = reversed_bits(((index // 2) * size + start) // block, bits) * block
            value = a[start : start + block, :].astype(F32) + b[start : start + block, :].astype(F32)
            out[to : to + block, cols] = value.astype(BF)


def add_stack(place, mine, theirs, bits):
    rows, half = mine[0].shape
    return launch(
        functools.partial(add_stack_kernel, len(mine), bits),
        "add",
        1,
        scalars(place) + whole(*mine, *theirs),
        [out_full((rows * len(mine) // 2, 2 * half))],
        [],
        4,
        32,
    )[0]


def spread_steps(value, bits):
    for step in reversed(range(1, len(bits))):
        got = yield [swap_dp(value, 1 << step)]
        value = ordered(value, got[0], bits[step])
    got = yield [swap_dp(value, 1)]
    yield value, got[0]


class Chain:
    def __init__(self, steps):
        self.steps = steps
        self.held = None

    def advance(self):
        try:
            self.held = self.steps.send(self.held)
            return True
        except StopIteration:
            return False

    def finish(self):
        while self.advance():
            pass
        return self.held


def pin(anchor, *chains):
    for chain in chains:
        chain.advance()
    held = lax.optimization_barrier((anchor, [chain.held for chain in chains]))
    for chain, value in zip(chains, held[1]):
        chain.held = value
    return held[0]


def shards(
    inputs,
    history,
    segment_ids,
    cotangent,
    input_weight,
    input_bias,
    merge_weight,
    merge_bias,
    first_gain,
    first_shift,
    second_gain,
    second_shift,
    expand_weight,
    expand_bias,
    reduce_weight,
    reduce_bias,
    depth_weights,
):
    member = lax.axis_index("mp")
    row, core = member // 2, member % 2
    dp = lax.axis_index("dp")
    bits = []
    size = lax.axis_size("dp")
    while (1 << len(bits)) < size:
        bits.append((dp >> len(bits)) & 1)
    bit = bits[0]
    flip = row ^ bit
    length = segment_ids.shape[1]
    part = inputs.shape[0]
    width = 4 * part
    half = width // 2
    units = expand_bias.shape[1]
    last = HISTORY - 1

    segments = lax.dynamic_slice_in_dim(segment_ids, row, 1, 0).astype(F32)
    frequency = 10000.0 ** (-jnp.arange(HALF, dtype=F32) * 2.0 / HEAD)
    angles = frequency[:, None] * jnp.arange(length, dtype=F32)[None, :]
    cos, sin = jnp.cos(angles), jnp.sin(angles)

    mine_at, sent_at = 2 * flip + core, 2 * (1 - flip) + core
    place = jnp.stack([bit, row, flip, core, mine_at, sent_at]).reshape(1, 6).astype(jnp.int32)
    attn_low = cast_weights(place, 0, ("attn",), (input_weight, merge_weight))
    attn_near, first_inputs = lax.optimization_barrier((attn_low[0][0], inputs))
    attn_w = [Weight(attn_near, attn_low[0][1])]
    attn_w[0].chain.advance()
    x0_low = split_rows(place, first_inputs)
    small = jnp.concatenate(
        [item.reshape(LAYERS, -1, part) for item in (input_bias, expand_bias)]
        + [
            item.reshape(LAYERS, 1, part)
            for item in (first_gain, first_shift, second_gain, second_shift, merge_bias, reduce_bias)
        ],
        1,
    )
    small = jnp.pad(
        small, ((0, 0), (0, TABLE_ROWS - small.shape[1]), (0, TABLE_LANES - part))
    )
    feed_low = cast_weights(place, 0, ("expand", "reduce"), (expand_weight, reduce_weight))
    x0_low, small = lax.optimization_barrier((x0_low, small))
    x0_chain = Chain(gather_steps(*x0_low))
    x0_chain.advance()
    vector_chain = Chain(gather_steps(small, small))
    attn_w[0].chain.held, feed_near = lax.optimization_barrier(
        (attn_w[0].chain.held, [feed_low[0][0], feed_low[1][0]])
    )
    expand_w = [Weight(feed_near[0], feed_low[0][1])]
    expand_w[0].chain.advance()
    reduce_w = [Weight(feed_near[1], feed_low[1][1])]
    vectors = vector_chain.finish()
    x0_chain.advance()
    x0_chain.held, late_weights, late_history = lax.optimization_barrier(
        (x0_chain.held, (input_weight, merge_weight, expand_weight, reduce_weight), history)
    )
    later = cast_weights(place, 1, ("attn", "expand", "reduce"), late_weights)
    hm_low = split_rows(place, late_history, depth_weights)
    x0 = x0_chain.finish()
    x0[0], later, hm_low = lax.optimization_barrier((x0[0], later, hm_low))
    attn_w.append(Weight(*later[0]))
    expand_w.append(Weight(*later[1]))
    reduce_w.append(Weight(*later[2], relay=False))
    hm0 = Chain(gather_steps(*hm_low))
    cot_chain = Chain(gather_steps(*split_rows(place, cotangent)))
    at = 3 * part + units

    saved = []
    mix = None
    for l in range(LAYERS):
        outs = attention_forward(
            place, mix, x0 if l == 0 else hm0, vectors, l, attn_w[l].parts(), cos, sin, segments
        )
        if l == 1:
            y0 = outs[0]
            outs = outs[1:]
        x = outs[0]
        outs = outs[1:]
        n1, st1, q, k, v, o, lse = outs[:7]
        left = list(outs[7:])
        if l == 0:
            left[0] = pin(left[0], expand_w[0].chain, reduce_w[0].chain)
        else:
            left[0] = pin(left[0], expand_w[1].chain, reduce_w[1].chain)
        right = swap_pieces(left)
        if l == 0:
            right[0] = pin(right[0], attn_w[1].chain)
            mid, n2, st2, u, act = mlp_forward(
                place, x, left, right, vectors, l, expand_w[0].parts(), None
            )
            act = pin(act, reduce_w[0].chain, hm0)
            left = list(reduce_forward(act, reduce_w[0].parts()))
            left[0] = pin(left[0], attn_w[1].chain)
            hm0 = hm0.finish()
            right = swap_pieces(left)
            right[0] = pin(right[0], expand_w[1].chain)
        else:
            mid, n2, st2, u, act, *left = mlp_forward(
                place, x, left, right, vectors, l, expand_w[1].parts(), reduce_w[1].parts()
            )
            left[0] = pin(left[0], cot_chain)
            right = swap_pieces(left)
        saved.append((x, n1, st1, (q, k, v, o, lse), mid, n2, st2, u, act, left, right))
        mix = (depth_weights, mid, *left, *right)

    cot = cot_chain.finish()
    def quarter_of(value, index):
        return lax.dynamic_slice_in_dim(value, index * part, part, 0)

    chains = [{} for _ in range(LAYERS)]
    sums = [{} for _ in range(LAYERS)]
    for l in reversed(range(LAYERS)):
        x, n1, st1, heads, mid, n2, st2, u, act, y_left, y_right = saved[l]
        aw, ew, rw = attn_w[l], expand_w[l], reduce_w[l]
        count = 2
        if l == 1:
            opening = (depth_weights, mid, *y_left, *y_right, y0, *vectors, *cot)
            gyb, cot, tail, wide_sums, dots1, *grads = mlp_backward(
                place, 1, False, "last", opening, None, n2, u, act, 1, rw.other(), ew.other(), None
            )
        else:
            opening = (
                (depth_weights, cot, gmb, saved[1][0], saved[1][2], *left, *right, y0, *vectors)
            )
            gyb, gx1, wide_sums, dots0, *grads = mlp_backward(
                place, 1, False, "first", opening, None, n2, u, act, 1, rw.other(), ew.other(), None
            )
            chains[1]["attn"].advance()
            gyb = pin(gyb, chains[1]["attn"])
            sums[1]["gain1"], sums[1]["shift1"] = (wide_sums, 8), (wide_sums, 16)
        sums[l]["reduce_b"] = (wide_sums, 0)
        e_other, r_other = grads[:count], grads[count : 2 * count]
        be1, partial = grads[2 * count :]
        *grads, be0, l0, l1, l2, l3 = mlp_backward(
            place, l, False, "own", None, gyb, n2, u, act, 0, rw.own, ew.own, partial
        )
        e_own, r_own, left = grads[:count], grads[count:], [l0, l1, l2, l3]
        if l == 1:
            right = swap_pieces(left)
            feed_own = r_own + e_own
            chains[1]["feed"] = Chain(half_steps(r_other + e_other))
            right[0] = pin(right[0], chains[1]["feed"])
        else:
            chains[l]["reduce"] = Chain(reduce_steps(r_own, r_other, bits))
            chains[l]["expand"] = Chain(reduce_steps(e_own, e_other, bits))
            left[0] = pin(left[0], chains[l]["reduce"], chains[1]["attn"])
            right = swap_pieces(left)
            right[0] = pin(right[0], chains[l]["reduce"])
        opening = (gyb, *left, *right, mid, st2, *vectors)
        gmb, wide_sums, *grads, db1, partial = attention_backward(
            place, l, False, opening, None, n1, aw.other(), cos, sin, segments, heads, 1, None
        )
        a_other = grads
        sums[l]["gain2"], sums[l]["shift2"], sums[l]["merge_b"] = (
            (wide_sums, 0),
            (wide_sums, 8),
            (wide_sums, 16),
        )
        if l == 1:
            gmb = pin(gmb, chains[1]["feed"])
        else:
            chains[0]["expand"].advance()
            gmb = pin(gmb, chains[l]["reduce"], chains[l]["expand"], chains[1]["attn"])
            gmb, sums_1 = lax.optimization_barrier((gmb, sums_1))
            chains[1]["feed"] = Chain(spread_steps(sums_1, bits))
        *grads, db0, l0, l1, l2, l3 = attention_backward(
            place, l, False, None, gmb, n1, aw.own, cos, sin, segments, heads, 0, partial
        )
        left = [l0, l1, l2, l3]
        chains[l]["attn"] = Chain(reduce_steps(grads, a_other, bits))
        if l == 0:
            chains[0]["attn"].advance()
            left[0] = pin(
                left[0],
                chains[0]["reduce"],
                chains[0]["expand"],
                chains[1]["attn"],
                chains[0]["attn"],
                chains[1]["feed"],
            )
        else:
            right = swap_pieces(left)
            chains[1]["feed"].advance()
            right[0] = pin(right[0], chains[1]["feed"])
            sums_1 = add_stack(place, feed_own, chains[1]["feed"].held, len(bits))
            sums_1 = lax.psum_scatter(sums_1, "dp", scatter_dimension=0, tiled=True)
        sums[l]["pair"] = ((db0, be0), (db1, be1))
    final = chains[0]["attn"]
    ahead = (chains[0]["reduce"], chains[0]["expand"], chains[1]["attn"], chains[1]["feed"])

    def onward(*passing):
        final.advance()
        for chain in ahead:
            chain.advance()
        final.held, held, passing = lax.optimization_barrier(
            (final.held, [chain.held for chain in ahead], passing)
        )
        for chain, value in zip(ahead, held):
            chain.held = value
        return passing

    right = swap_pieces(left)
    gx1, tail = lax.optimization_barrier((left[0], (gx1, tail)))[1]
    homes = [
        Chain(home_steps(quarter_of(item, mine_at), quarter_of(item, sent_at), row))
        for item in (gx1, tail)
    ]
    for home in homes:
        home.advance()
    final.advance()
    chains[0]["reduce"].advance()
    chains[1]["attn"].advance()
    chains[1]["feed"].advance()
    gx0, wide_sums = final_backward(
        place, gmb, saved[0][0], saved[0][2], *left, *right, *vectors
    )
    sums[0]["gain1"], sums[0]["shift1"] = (wide_sums, 0), (wide_sums, 8)

    final.held, held, homes[0].held, homes[1].held, gx0 = lax.optimization_barrier(
        (final.held, [chain.held for chain in ahead], homes[0].held, homes[1].held, gx0)
    )
    for chain, value in zip(ahead, held):
        chain.held = value
    homes.append(Chain(home_steps(quarter_of(gx0, mine_at), quarter_of(gx0, sent_at), row)))
    homes[2].advance()
    pairs = [found.pop("pair") for found in sums]
    row_at = [{name: at for name, (_, at) in found.items()} for found in sums]
    held_sums = [{name: item for name, (item, _) in found.items()} for found in sums]
    late_cot, past, held_sums, pairs, dots0, dots1, homes[2].held = onward(
        cotangent, history, held_sums, pairs, dots0, dots1, homes[2].held
    )
    output, input_grad, history_out, dots = finish(
        place, depth_weights, past, late_cot, *[home.finish() for home in (homes[1], homes[0], homes[2])]
    )
    output, input_grad, history_out, dots = onward(output, input_grad, history_out, dots)
    entry_dots = jnp.sum(dots[:, ::4], 2)

    def by_core(value):
        return jnp.where(core == 0, jnp.sum(value), 0.0)

    mix_sum = jnp.concatenate(
        [
            entry_dots[:, 0],
            by_core(dots0[0])[None],
            entry_dots[1:, 1],
            by_core(dots1[0])[None],
            by_core(dots1[1])[None],
        ]
    )
    mix_sum = mix_sum + swap_core(mix_sum)

    names = ("gain1", "shift1", "gain2", "shift2", "merge_b", "reduce_b")

    wide = [(held_sums[l][name], row_at[l][name]) for l in range(LAYERS) for name in names]
    flat_pairs = [pairs[l][which][k] for l in range(LAYERS) for which in range(2) for k in range(2)]
    lines = vector_lines(
        place, wide, flat_pairs, jnp.pad(mix_sum, (0, 128 - mix_sum.shape[0]))[None], width, part
    )
    total = lines[0] + swap_row(lines[1])
    (total,) = onward(total)
    for step in range(len(bits)):
        total = total + swap_dp(total, 1 << step)
    at = LAYERS * 6
    mix_grad = total[at + 2 * LAYERS, : mix_sum.shape[0]].reshape(LAYERS, HISTORY + 1)
    wide_out = [total[i:at:6, :part] for i in range(6)]
    input_out = total[at : at + 2 * LAYERS : 2, : 3 * part].reshape(LAYERS, 3, part)
    expand_out = total[at + 1 : at + 2 * LAYERS : 2, :units]

    attn_t = expand_t = reduce_t = None
    for l in reversed(range(LAYERS)):
        if l == 0:
            total = [chains[l][name].finish() for name in ("reduce", "expand", "attn")]
        else:
            feed = chains[1]["feed"].finish()
            total = [(feed, 0), (feed, 1), chains[1]["attn"].finish()]
        reduce_t = assemble(total[0], place, l, [(LAYERS, units, width)], [units], False, reduce_t)
        expand_t = assemble(total[1], place, l, [(LAYERS, width, units)], [units], True, expand_t)
        attn_t = assemble(
            total[2],
            place,
            l,
            [(LAYERS, 3, part, width), (LAYERS, part, width)],
            [3 * part, part],
            False,
            attn_t,
        )
    return (
        output,
        input_grad,
        history_out,
        attn_t[0],
        input_out,
        attn_t[1],
        wide_out[4],
        wide_out[0],
        wide_out[1],
        wide_out[2],
        wide_out[3],
        expand_t[0],
        expand_out,
        reduce_t[0],
        wide_out[5],
        mix_grad,
    )


def solution(mesh):
    in_specs = (
        P("mp", "dp"),
        P(None, "mp", "dp"),
        P("dp", None),
        P("mp", "dp"),
        P(None, None, "mp", None),
        P(None, None, "mp"),
        P(None, "mp", None),
        P(None, "mp"),
        P(None, "mp"),
        P(None, "mp"),
        P(None, "mp"),
        P(None, "mp"),
        P(None, None, "mp"),
        P(None, "mp"),
        P(None, "mp", None),
        P(None, "mp"),
        P(),
    )
    out_specs = (
        P("mp", "dp"),
        P("mp", "dp"),
        P(None, "mp", "dp"),
        P(None, None, "mp", None),
        P(None, None, "mp"),
        P(None, "mp", None),
        P(None, "mp"),
        P(None, "mp"),
        P(None, "mp"),
        P(None, "mp"),
        P(None, "mp"),
        P(None, None, "mp"),
        P(None, "mp"),
        P(None, "mp", None),
        P(None, "mp"),
        P(),
    )
    return jax.shard_map(shards, mesh=mesh, in_specs=in_specs, out_specs=out_specs, check_vma=False)
```
